128 devices in a mesh: dp: 8 (over y, core), ctx: 16 (over x, z).
Axes of the slice: x: 4, y: 4, z: 4, core: 2. Of those that a mesh axis runs over, the one named last changes fastest.
Arguments:
- tokens: bfloat16 [8, 16384, 768], P('dp', 'ctx'), may hold values from -6 to 6
- kept: int32 [8], P('dp'), may hold values from 2048 to 16384, as said below
- gain: float32 [768], replicated, may hold values from 0.25 to 1.75
- w_qkv: bfloat16 [768, 2304], replicated, may hold values from -0.21875 to 0.21875
- w_out: bfloat16 [768, 768], replicated, may hold values from -0.21875 to 0.21875
- grad_out: bfloat16 [8, 16384, 768], P('dp', 'ctx'), may hold values from -6 to 6
Outputs:
- layer_out: bfloat16 [8, 16384, 768], P('dp', 'ctx')
- grad_tokens: bfloat16 [8, 16384, 768], P('dp', 'ctx')
- grad_qkv: float32 [768, 2304], replicated
- grad_proj: float32 [768, 768], replicated
- gain_gradient: float32 [768], replicated
The draws below stay inside these ranges and needn't reach their ends.
Inputs may be any that keep to these rules, and one draw needn't show every extreme that they name: Some slide of every draw is full, kept = 16384.
All inputs are finite; a program needn't handle non-finite values.
Results may differ from the reference program's by a relative error of at most 0.0093.
Values may be sent and summed in bfloat16 or wider, within the bound.
A program may use at most 128 MiB of HBM per device.

```python
import jax
import jax.numpy as jnp
import numpy as np
from jax import lax

D = 768
HEADS = 12
TOK_DEV = 1024
CAP = 16384
SLIDES = 8
N_CTX = 16


def draw_kept(key, part):
    key = jax.random.fold_in(key, 7)
    first, second = jax.random.split(key)
    counts = jax.random.randint(first, (SLIDES,), 2 * TOK_DEV, CAP + 1)
    chosen = jax.random.randint(second, (), 0, SLIDES)
    return jnp.where(jnp.arange(SLIDES) == chosen, CAP, counts).astype(jnp.int32)


def levels(stream_key, dims, cuts, low, high):
    def one(axis_at, blocks):
        steps = jax.random.uniform(jax.random.fold_in(jax.random.fold_in(stream_key, 6), axis_at), (blocks,), jnp.float32, low / len(cuts), high / len(cuts))
        return jnp.repeat(jnp.exp(steps), dims[axis_at] // blocks).reshape((-1,) + (1,) * (len(dims) - axis_at - 1))

    level = one(*cuts[0])
    for cut in cuts[1:]:
        level = level * one(*cut)
    return level


def normal_values(stream_key, shape, scale, most, cuts=(), held_as=jnp.bfloat16):
    array = jax.random.normal(stream_key, shape, jnp.float32) * scale
    if len(cuts) > 0:
        array = levels(stream_key, shape, cuts, -0.22, 0.18) * array
    return jnp.clip(array, min=-most, max=most).astype(held_as)


def setup_inputs(seed: int = 0) -> dict:
    splits = jax.random.split(jax.random.key(seed), 7)
    tokens = normal_values(splits[0], (SLIDES, CAP, D), 1.0, 6.0, ((0, 8), (1, 16)))
    kept = draw_kept(jax.random.fold_in(splits[6], 71), 0)
    gain = jnp.clip(1.0 + 0.15 * jax.random.normal(splits[2], (D,), jnp.float32), 0.25, 1.75)
    w_qkv = normal_values(splits[3], (D, 3 * D), D ** -0.5, 0.21875)
    w_out = normal_values(splits[4], (D, D), D ** -0.5, 0.21875)
    grad_out = normal_values(splits[5], (SLIDES, CAP, D), 1.0, 6.0, ((0, 8), (1, 16)))
    return dict(tokens=tokens, kept=kept, gain=gain, w_qkv=w_qkv, w_out=w_out, grad_out=grad_out)


def pick_rows(values, rate, group):
    offsets = np.arange(group) % rate
    columns = np.arange(group)
    shaped = values.reshape((values.shape[0] // rate, rate) + values.shape[1:])
    return shaped[:, offsets, columns]

def place_rows(chosen, rate, group):
    offsets = np.arange(group) % rate
    columns = np.arange(group)
    token_rows = chosen.shape[0]
    empty = jnp.zeros((token_rows, rate) + chosen.shape[1:], chosen.dtype)
    return empty.at[:, offsets, columns].set(chosen).reshape((token_rows * rate,) + chosen.shape[1:])

def narrow(values):
    return lax.optimization_barrier(values.astype(jnp.bfloat16)).astype(jnp.float32)

def masked_scores(queries, keys, key_valid, scale):
    raw = jnp.einsum('bqgd,bkgd->bgqk', queries.astype(jnp.float32), keys.astype(jnp.float32)) * scale
    return jnp.where(jnp.transpose(key_valid, (0, 2, 1))[:, :, None, :], raw, -1000000000.0)

def attend_forward(queries, keys, values, key_valid, query_valid, scale):
    scores = masked_scores(queries, keys, key_valid, scale)
    peak = lax.optimization_barrier(jnp.max(scores, -1, keepdims=True))
    log_total = peak[..., 0] + jnp.log(lax.optimization_barrier(jnp.sum(jnp.exp(scores - peak), -1)))
    weights = jnp.exp(scores - log_total[..., None]).astype(jnp.bfloat16)
    mixed = jnp.einsum('bgqk,bkgd->bqgd', weights.astype(jnp.float32), values.astype(jnp.float32))
    output = jnp.where(query_valid[..., None], mixed, 0.0).astype(jnp.bfloat16)
    return (output, log_total)

def attend_backward(queries, keys, values, key_valid, grad_output, log_total, inner, scale):
    scores = masked_scores(queries, keys, key_valid, scale)
    weights = jnp.exp(scores - log_total[..., None])
    grad_weights = jnp.einsum('bqgd,bkgd->bgqk', grad_output.astype(jnp.float32), values.astype(jnp.float32))
    grad_scores = (weights * (grad_weights - inner[..., None]) * scale).astype(jnp.bfloat16).astype(jnp.float32)
    grad_q = jnp.einsum('bgqk,bkgd->bqgd', grad_scores, keys.astype(jnp.float32))
    grad_k = jnp.einsum('bgqk,bqgd->bkgd', grad_scores, queries.astype(jnp.float32))
    grad_v = jnp.einsum('bgqk,bqgd->bkgd', narrow(weights), grad_output.astype(jnp.float32))
    return (grad_q, grad_k, grad_v)

def row_inner(grad_output, output):
    total = lax.optimization_barrier(jnp.sum(grad_output.astype(jnp.float32) * output.astype(jnp.float32), -1))
    return jnp.transpose(total, (0, 2, 1))

def apply_layer_norm(token_rows, gain):
    wide = token_rows.astype(jnp.float32)
    centered_input = wide - lax.optimization_barrier(jnp.mean(wide, -1, keepdims=True))
    inverse_deviation = lax.rsqrt(lax.optimization_barrier(jnp.mean(centered_input * centered_input, -1, keepdims=True)) + 1e-05)
    standardized_input = centered_input * inverse_deviation
    return ((standardized_input * gain).astype(jnp.bfloat16), standardized_input, inverse_deviation)

def slide_pass(token_rows, grad_rows, limit, gain, w_qkv, w_out):
    length, width = token_rows.shape
    group = HEADS // 3
    size = width // HEADS
    scale = size ** (-0.5)
    normalized_rows, standardized_input, inverse_deviation = apply_layer_norm(token_rows, gain)
    qkv = jnp.dot(normalized_rows, w_qkv, preferred_element_type=jnp.float32).astype(jnp.bfloat16)
    qkv = qkv.reshape(length, 3, 3, group, size)
    valid = jnp.arange(length) < limit
    wide_valid = jnp.broadcast_to(valid[:, None], (length, group))
    rates = (1, 2, N_CTX)
    outputs = []
    saved = []
    for level in range(3):
        rate = rates[level]
        parts = [pick_rows(qkv[:, kind, level], rate, group).reshape(-1, TOK_DEV, group, size) for kind in range(3)]
        mask = pick_rows(wide_valid, rate, group).reshape(-1, TOK_DEV, group)
        output, log_total = attend_forward(parts[0], parts[1], parts[2], mask, mask, scale)
        outputs.append(place_rows(output.reshape(-1, group, size), rate, group))
        saved.append((parts, mask, output, log_total))
    attn = jnp.stack(outputs, 1).reshape(length, width)
    layer = (token_rows.astype(jnp.float32) + jnp.dot(attn, w_out, preferred_element_type=jnp.float32)).astype(jnp.bfloat16)
    grad_proj = jnp.dot(attn.T, grad_rows, preferred_element_type=jnp.float32)
    grad_attn = jnp.dot(grad_rows, w_out.T, preferred_element_type=jnp.float32).astype(jnp.bfloat16)
    grad_attn = grad_attn.reshape(length, 3, group, size)
    placed = []
    for level in range(3):
        rate = rates[level]
        parts, mask, output, log_total = saved[level]
        grad_output = pick_rows(grad_attn[:, level], rate, group).reshape(-1, TOK_DEV, group, size)
        grad_output = jnp.where(mask[..., None], grad_output, jnp.zeros_like(grad_output))
        inner = row_inner(grad_output, output)
        grads = attend_backward(parts[0], parts[1], parts[2], mask, grad_output, log_total, inner, scale)
        placed.append([place_rows(item.reshape(-1, group, size), rate, group) for item in grads])
    stacked = jnp.stack([jnp.stack([placed[level][kind] for level in range(3)], 1) for kind in range(3)], 1)
    grad_qkv_rows = stacked.reshape(length, 3 * width).astype(jnp.bfloat16)
    grad_weight = jnp.dot(normalized_rows.T, grad_qkv_rows, preferred_element_type=jnp.float32)
    normalized_gradient = jnp.dot(grad_qkv_rows, w_qkv.T, preferred_element_type=jnp.float32)
    gain_gradient = lax.optimization_barrier(jnp.sum(normalized_gradient * standardized_input, 0))
    rescaled_rows = normalized_gradient * gain
    input_gradient = inverse_deviation * (rescaled_rows - lax.optimization_barrier(jnp.mean(rescaled_rows, -1, keepdims=True)) - standardized_input * lax.optimization_barrier(jnp.mean(rescaled_rows * standardized_input, -1, keepdims=True)))
    grad_tokens = (grad_rows.astype(jnp.float32) + input_gradient).astype(jnp.bfloat16)
    return (layer, grad_tokens, grad_weight, grad_proj, gain_gradient)

def reference(tokens, kept, gain, w_qkv, w_out, grad_out):

    def one_slide(items):
        return slide_pass(items[0], items[1], items[2], gain, w_qkv, w_out)
    layer, grad_tokens, grad_weight, grad_proj, gain_gradient = lax.map(one_slide, (tokens, grad_out, kept))
    return (layer, grad_tokens, lax.optimization_barrier(jnp.sum(grad_weight, 0)), lax.optimization_barrier(jnp.sum(grad_proj, 0)), lax.optimization_barrier(jnp.sum(gain_gradient, 0)))
```

```python
import functools

import jax
import jax.numpy as jnp
import numpy as np
from jax import lax
from jax.experimental import pallas as pl
from jax.experimental.pallas import tpu as pltpu
from jax.sharding import PartitionSpec as P

BF = jnp.bfloat16
F32 = jnp.float32
LOG2E = 1.4426950408889634
Q_SCALE = 0.125 * LOG2E
NEG = -1e9
R = 1024
D = 768
BLK = 256
VMEM = 60 * 1024 * 1024


def nn(a, b):
    return lax.dot_general(a, b, (((1,), (0,)), ((), ())), preferred_element_type=F32)


def nt(a, b):
    return lax.dot_general(a, b, (((1,), (1,)), ((), ())), preferred_element_type=F32)


def iota(shape, dim):
    return lax.broadcasted_iota(jnp.int32, shape, dim)


def residue(i):
    return jnp.where(i < 8, 2 * i, 2 * i - 15)


def place(p):
    return 16 * (p & 63) + residue(p >> 6)


def row_order():
    r, c = iota((256, 256), 0), iota((256, 256), 1)
    return jnp.where(c == 16 * (r & 15) + residue(r >> 4), 1.0, 0.0).astype(BF)


def row_order_back():
    c, r = iota((256, 256), 0), iota((256, 256), 1)
    return jnp.where(c == 16 * (r & 15) + residue(r >> 4), 1.0, 0.0).astype(BF)


def head_order():
    r, c = iota((256, 256), 0), iota((256, 256), 1)
    b = c >> 6
    b = jnp.where(b == 1, 2, jnp.where(b == 2, 1, b))
    return jnp.where(r == 64 * b + (c & 63), 1.0, 0.0).astype(BF)


HEAD_BLOCKS = (0, 2, 1, 3)


def split_diag(x):
    left = iota((64, 128), 1) < 64
    return jnp.where(left, x[:64], x[64:])


def diag_mask(x):
    r, c = iota((128, 128), 0), iota((128, 128), 1)
    return jnp.where((r < 64) == (c < 64), x, 0.0)


def project(
    kept, tokens, gain, w, w_out, grad_out,
    xp, gp, nm, nmt, wp, wo, q0t, k0, v0, q1t, k1, v1, q2t, kv2, do0, do1, do2,
):
    base = lax.axis_index("ctx") * R
    limit = kept[0] - base
    order = row_order()
    for t in range(4):
        rows = slice(256 * t, 256 * t + 256)
        x = nn(order, tokens[rows])
        mean = jnp.mean(x, -1, keepdims=True)
        cent = x - mean
        inv = lax.rsqrt(jnp.mean(cent * cent, -1, keepdims=True) + 1e-05)
        n = (cent * inv * gain[...]).astype(BF)
        xb = x.astype(BF)
        gb = nn(order, grad_out[rows]).astype(BF)
        for i in range(16):
            to = slice(64 * i + 16 * t, 64 * i + 16 * t + 16)
            fr = slice(16 * i, 16 * i + 16)
            xp[to] = xb[fr]
            gp[to] = gb[fr]
            nm[to] = n[fr]
    heads = head_order()
    for level in (1, 2):
        for kind in range(3):
            cols = w[:, kind * D + level * 256 : kind * D + level * 256 + 256]
            wp[:, (level - 1) * D + kind * 256 : (level - 1) * D + kind * 256 + 256] = nn(cols, heads).astype(BF)
    wo[:256] = w_out[:256]
    for level in (1, 2):
        for at, block in enumerate(HEAD_BLOCKS):
            wo[256 * level + 64 * at : 256 * level + 64 * at + 64] = w_out[256 * level + 64 * block : 256 * level + 64 * block + 64]
    for half in range(2):
        rows = slice(512 * half, 512 * half + 512)
        few = slice(512 * half, 512 * half + 128)
        lanes = [slice(256 * kind + 128 * half, 256 * kind + 128 * half + 128) for kind in range(6)]
        k1[rows] = nn(nm[rows], wp[:, lanes[1]]).astype(BF)
        v1[rows] = nn(nm[rows], wp[:, lanes[2]]).astype(BF)
        kv2[2 * half] = split_diag(nn(nm[few], wp[:, lanes[4]])).astype(BF)
        kv2[2 * half + 1] = split_diag(nn(nm[few], wp[:, lanes[5]])).astype(BF)
        q1t[half] = jnp.transpose(nn(nm[rows], wp[:, lanes[0]]) * Q_SCALE).astype(BF)
        q2t[half] = jnp.transpose(diag_mask(nn(nm[few], wp[:, lanes[3]])) * Q_SCALE).astype(BF)
        cols = iota((1, 512), 1) + 512 * half
        ok = place(cols) < limit
        do1[half] = jnp.where(ok, nt(wo[256 + 128 * half : 384 + 128 * half], gp[rows]), 0.0).astype(BF)
        cols = iota((1, 128), 1) + 512 * half
        ok = place(cols) < limit
        do2[half] = jnp.where(ok, diag_mask(nt(wo[512 + 128 * half : 640 + 128 * half], gp[few])), 0.0).astype(BF)
    for t in range(4):
        rows = slice(256 * t, 256 * t + 256)
        q0t[:, rows] = jnp.transpose(nn(nm[rows], w[:, :256]) * Q_SCALE).astype(BF)
        k0[rows] = nn(nm[rows], w[:, D : D + 256]).astype(BF)
        v0[rows] = nn(nm[rows], w[:, 2 * D : 2 * D + 256]).astype(BF)
        ok = place(iota((1, 256), 1) + 256 * t) < limit
        do0[:, rows] = jnp.where(ok, nt(wo[:256], gp[rows]), 0.0).astype(BF)
        nmt[:, rows] = jnp.transpose(nm[rows])


def prepare_pair(k, v, bias, ka, va, vat, kt):
    lane = iota((R, 128), 1)
    for h in range(2):
        mine = (lane < 64) == (h == 0)
        other = 64 - 64 * h
        ka[h] = jnp.where(mine, k.astype(F32), jnp.where(lane == other, bias, 0.0)).astype(BF)
        both = (lane == other) | (lane == other + 1)
        va_h = jnp.where(mine, v.astype(F32), jnp.where(both, 1.0, 0.0))
        va[h] = va_h.astype(BF)
        vat[h] = jnp.transpose(va_h).astype(BF)
    kt[...] = jnp.transpose(k.astype(F32)).astype(BF)


def prepare_queries(qt, qa):
    sub = iota(qt.shape, 0)
    for h in range(2):
        mine = (sub < 64) == (h == 0)
        other = 64 - 64 * h
        qa[h, :, : qt.shape[1]] = jnp.where(mine, qt.astype(F32), jnp.where(sub == other, 1.0, 0.0)).astype(BF)


def attend_block(h, first, cols, ok, qa, dot_, ka, va, vat, kt, dk, dv, s_ref, p_ref):
    head = slice(64 * h, 64 * h + 64)
    other = 64 - 64 * h
    q = qa[h, :, cols]
    top = None
    for c in range(4):
        keys = slice(256 * c, 256 * c + 256)
        s = nn(ka[h, keys], q)
        s_ref[h, keys] = s
        m = jnp.max(s, 0, keepdims=True)
        top = m if top is None else jnp.maximum(top, m)
    o = None
    for c in range(4):
        keys = slice(256 * c, 256 * c + 256)
        p = jnp.exp2(s_ref[h, keys] - top).astype(BF)
        p_ref[h, keys] = p
        part = nn(vat[h, :, keys], p)
        o = part if o is None else o + part
    scale = 1.0 / o[other : other + 1]
    out = jnp.where(ok, o[head] * scale, 0.0).astype(BF)
    do = dot_.astype(F32)
    inner = jnp.sum(do * out.astype(F32), 0, keepdims=True) * scale
    high = inner.astype(BF).astype(F32)
    low = inner - high
    sub = iota((64, BLK), 0)
    extra = jnp.where(sub == 0, -high, jnp.where(sub == 1, -low, 0.0))
    parts = [do * scale, extra] if h == 0 else [extra, do * scale]
    da = jnp.concatenate(parts, 0).astype(BF)
    dq = None
    for c in range(4):
        keys = slice(256 * c, 256 * c + 256)
        dp = nn(va[h, keys], da)
        p = p_ref[h, keys]
        ds = (p.astype(F32) * dp).astype(BF)
        dv_new = nt(p, da)
        dk_new = nt(ds, q)
        if first is None:
            dv[h, keys] = dv_new
            dk[h, keys] = dk_new
        else:
            dv[h, keys] += dv_new
            dk[h, keys] += dk_new
        part = nn(kt[head, keys], ds)
        dq = part if dq is None else dq + part
    return out, (dq * 0.125).astype(BF)


def join(acc, scale):
    lane = iota((acc.shape[1], 128), 1)
    return jnp.where(lane < 64, acc[0], acc[1]) * scale


def attend_pair(qt, dot_, k, v, bias, limit, start, width, outs, dqs, scr):
    ka, va, vat, kt, qa, dk, dv, s_ref, p_ref = scr
    prepare_pair(k, v, bias, ka, va, vat, kt)
    prepare_queries(qt[...], qa)
    dk[...] = jnp.zeros_like(dk)
    dv[...] = jnp.zeros_like(dv)

    def step(i, _):
        cols = pl.ds(pl.multiple_of(i * BLK, BLK), BLK)
        ok = place(iota((1, BLK), 1) + start + i * BLK) < limit
        for h in range(2):
            head = slice(64 * h, 64 * h + 64)
            o, dq = attend_block(h, i, cols, ok, qa, dot_[head, cols], ka, va, vat, kt, dk, dv, s_ref, p_ref)
            outs[head, cols] = o
            dqs[head, cols] = dq
        return 0

    lax.fori_loop(0, width // BLK, step, 0)


def attend_few(qd, do, k, v, bias, ok):
    s = nn(k, qd) + bias
    top = jnp.max(s, 0, keepdims=True)
    p = jnp.exp2(s - top).astype(BF)
    pf = p.astype(F32)
    scale = 1.0 / jnp.sum(pf, 0, keepdims=True)
    o = nn(jnp.transpose(v.astype(F32)).astype(BF), p) * scale
    o = jnp.where(ok, diag_mask(o), 0.0).astype(BF)
    do32 = do.astype(F32)
    inner = jnp.sum(do32 * o.astype(F32), 0, keepdims=True) * scale
    da = (do32 * scale).astype(BF)
    ds = (pf * (nn(v, da) - inner)).astype(BF)
    dq = diag_mask(nn(jnp.transpose(k.astype(F32)).astype(BF), ds)) * 0.125
    return o, dq.astype(BF), nt(ds, qd) * (1.0 / LOG2E), nt(p, da)


def attend(
    kept, q0t, k0, v0, q1t, k1, v1, far1, q2t, kv2, do0, do1, do2,
    o0, o1, o2, dq0, dq1, dq2, dk0, dv0, near, back, back2,
    ka, va, vat, kt, qa, dk, dv, s_ref, p_ref,
):
    me = lax.axis_index("ctx")
    base = me * R
    limit = kept[0] - base
    far_limit = kept[0] - (me ^ 1) * R
    scr = (ka, va, vat, kt, qa, dk, dv, s_ref, p_ref)
    sub = iota((R, 128), 0)
    lane = iota((R, 128), 1)
    bias = jnp.where(place(sub) < limit, 0.0, NEG)
    for pair in range(2):
        c = slice(128 * pair, 128 * pair + 128)
        attend_pair(q0t.at[c], do0.at[c], k0[:, c], v0[:, c], bias, limit, 0, R, o0.at[c], dq0.at[c], scr)
        dk0[:, c] = join(dk, 1.0 / LOG2E).astype(BF)
        dv0[:, c] = join(dv, 1.0).astype(BF)
    for half in range(2):
        rows = slice(512 * half, 512 * half + 512)
        at = place((sub & 511) + 512 * half)
        bias = jnp.where(at < jnp.where(sub < 512, limit, far_limit), 0.0, NEG)
        k = jnp.concatenate([k1[rows], far1[0, rows]], 0)
        v = jnp.concatenate([v1[rows], far1[1, rows]], 0)
        attend_pair(q1t.at[half], do1.at[half], k, v, bias, limit, 512 * half, 512, o1.at[half], dq1.at[half], scr)
        gk = join(dk, 1.0 / LOG2E)
        gv = join(dv, 1.0)
        near[0, rows] = gk[:512]
        near[1, rows] = gv[:512]
        back[0, rows] = gk[512:].astype(BF)
        back[1, rows] = gv[512:].astype(BF)
    for half in range(2):
        at = R * (sub >> 6) + 16 * (sub & 63) + jnp.where(lane < 64, half, half + 2)
        bias = jnp.where(at < kept[0], 0.0, NEG)
        ok = place(iota((1, 128), 1) + 512 * half) < limit
        k = kv2[:, 2 * half].reshape(R, 128)
        v = kv2[:, 2 * half + 1].reshape(R, 128)
        o, dq, gk, gv = attend_few(q2t[half], do2[half], k, v, bias, ok)
        o2[half] = o
        dq2[half] = dq
        back2[:, 2 * half] = gk.astype(BF).reshape(16, 64, 128)
        back2[:, 2 * half + 1] = gv.astype(BF).reshape(16, 64, 128)


def spread(x):
    return diag_mask(jnp.concatenate([x, x], 0))


def finish(
    xp, gp, nmt, gain, w, wp, wo, o0, o1, o2, dq0, dq1, dq2, dk0, dv0, near, back, back2,
    layer, grad_tokens, gw, g0, g1, g2,
):
    def flip(x):
        return jnp.transpose(x.astype(F32)).astype(BF)

    for t in range(4):
        rows = slice(256 * t, 256 * t + 256)
        g0[rows, :256] = flip(dq0[:, rows])
    g0[:, 256:512] = dk0[...]
    g0[:, 512:768] = dv0[...]
    for half in range(2):
        rows = slice(512 * half, 512 * half + 512)
        g1[rows, :128] = flip(dq1[half])
        for kind in range(2):
            g1[rows, 128 + 128 * kind : 256 + 128 * kind] = (near[kind, rows] + back[kind, rows].astype(F32)).astype(BF)
        g2[half, :, :128] = flip(dq2[half])
        for kind in range(2):
            total = jnp.sum(back2[:, 2 * half + kind].astype(F32), 0)
            g2[half, :, 128 + 128 * kind : 256 + 128 * kind] = spread(total).astype(BF)
    for t in range(3):
        c = slice(256 * t, 256 * t + 256)
        gw[:, c] = nn(nmt[...], g0[:, c]).astype(BF)
    for half in range(2):
        rows = slice(512 * half, 512 * half + 512)
        few = slice(512 * half, 512 * half + 128)
        gw[:, 768 + 384 * half : 1152 + 384 * half] = nn(nmt[:, rows], g1[rows]).astype(BF)
        gw[:, 1536 + 384 * half : 1920 + 384 * half] = nn(nmt[:, few], g2[half]).astype(BF)
    gw[:256, 2304:] = nn(o0[...], gp[...]).astype(BF)
    for half in range(2):
        rows = slice(512 * half, 512 * half + 512)
        few = slice(512 * half, 512 * half + 128)
        gw[256 + 128 * half : 384 + 128 * half, 2304:] = nn(o1[half], gp[rows]).astype(BF)
        gw[512 + 128 * half : 640 + 128 * half, 2304:] = nn(o2[half], gp[few]).astype(BF)
    for t in range(8):
        rows = slice(128 * t, 128 * t + 128)
        half = t // 4
        at = slice(128 * (t % 4), 128 * (t % 4) + 128)
        lanes = [slice(256 * kind + 128 * half, 256 * kind + 128 * half + 128) for kind in range(6)]
        u = nt(g0[rows, :256], w[:, :256]) + nt(g0[rows, 256:512], w[:, D : D + 256]) + nt(g0[rows, 512:768], w[:, 2 * D : 2 * D + 256])
        y = nn(flip(o0[:, rows]), wo[:256]) + nn(flip(o1[half, :, at]), wo[256 + 128 * half : 384 + 128 * half])
        for kind in range(3):
            u += nt(g1[rows, 128 * kind : 128 * kind + 128], wp[:, lanes[kind]])
        if t % 4 == 0:
            for kind in range(3):
                u += nt(g2[half, :, 128 * kind : 128 * kind + 128], wp[:, lanes[3 + kind]])
            y += nn(flip(o2[half]), wo[512 + 128 * half : 640 + 128 * half])
        x = xp[rows].astype(F32)
        layer[rows] = (x + y).astype(BF)
        u = u * gain[...]
        cent = x - jnp.mean(x, -1, keepdims=True)
        inv = lax.rsqrt(jnp.mean(cent * cent, -1, keepdims=True) + 1e-05)
        xhat = cent * inv
        mean = jnp.mean(u, -1, keepdims=True)
        dotted = jnp.mean(u * xhat, -1, keepdims=True)
        grad_tokens[rows] = (gp[rows].astype(F32) + inv * (u - mean - xhat * dotted)).astype(BF)


def deliver(layer_p, tokens_p, gw, gain, w, layer, grad_tokens, g_qkv, g_proj, g_gain):
    order = row_order_back()
    for t in range(4):
        rows = slice(256 * t, 256 * t + 256)
        for src, dst in ((layer_p, layer), (tokens_p, grad_tokens)):
            x = jnp.concatenate([src[64 * i + 16 * t : 64 * i + 16 * t + 16] for i in range(16)], 0)
            dst[rows] = nn(order, x).astype(BF)
    heads = head_order()
    total = jnp.zeros((D, 128), F32)
    for kind in range(3):
        for level in range(3):
            if level == 0:
                x = gw[:, 256 * kind : 256 * kind + 256].astype(F32)
            else:
                at = 768 * level + 128 * kind
                x = nn(jnp.concatenate([gw[:, at : at + 128], gw[:, at + 384 : at + 512]], 1), heads)
            c = slice(D * kind + 256 * level, D * kind + 256 * level + 256)
            g_qkv[:, c] = x
            prod = x * w[:, c].astype(F32)
            total += prod[:, :128] + prod[:, 128:]
    g_gain[...] = jnp.sum(jnp.transpose(total), 0, keepdims=True) / gain[...]
    g_proj[:256] = gw[:256, 2304:].astype(F32)
    for level in (1, 2):
        for at, block in enumerate(HEAD_BLOCKS):
            g_proj[256 * level + 64 * block : 256 * level + 64 * block + 64] = gw[256 * level + 64 * at : 256 * level + 64 * at + 64, 2304:].astype(F32)


def shape(*dims, dtype=BF):
    return jax.ShapeDtypeStruct(dims, dtype)


V = pl.BlockSpec(memory_space=pltpu.VMEM)
S = pl.BlockSpec(memory_space=pltpu.SMEM)
PARAMS = pltpu.CompilerParams(vmem_limit_bytes=VMEM)


def shards(tokens, kept, gain, w, w_out, grad_out):
    x, g = tokens[0], grad_out[0]
    gain2 = gain[None]
    xp, gp, nm, nmt, wp, wo, q0t, k0, v0, q1t, k1, v1, q2t, kv2, do0, do1, do2 = pl.pallas_call(
        project,
        out_shape=[
            shape(R, D), shape(R, D), shape(R, D), shape(D, R), shape(D, 2 * D), shape(D, D),
            shape(256, R), shape(R, 256), shape(R, 256),
            shape(2, 128, 512), shape(R, 128), shape(R, 128), shape(2, 128, 128), shape(4, 64, 128),
            shape(256, R), shape(2, 128, 512), shape(2, 128, 128),
        ],
        in_specs=[S] + [V] * 5,
        out_specs=[V] * 17,
        compiler_params=PARAMS,
        name="project",
    )(kept, x, gain2, w, w_out, g)
    swap = [(i, i ^ 1) for i in range(lax.axis_size("ctx"))]
    far1 = lax.ppermute(jnp.stack([k1, v1]), "ctx", swap)
    kv2_all = lax.all_gather(kv2, "ctx", axis=0)
    o0, o1, o2, dq0, dq1, dq2, dk0, dv0, near, back, back2 = pl.pallas_call(
        attend,
        out_shape=[
            shape(256, R), shape(2, 128, 512), shape(2, 128, 128),
            shape(256, R), shape(2, 128, 512), shape(2, 128, 128),
            shape(R, 256), shape(R, 256),
            shape(2, R, 128, dtype=F32), shape(2, R, 128), shape(16, 4, 64, 128),
        ],
        in_specs=[S] + [V] * 12,
        out_specs=[V] * 11,
        scratch_shapes=[
            pltpu.VMEM((2, R, 128), BF), pltpu.VMEM((2, R, 128), BF), pltpu.VMEM((2, 128, R), BF),
            pltpu.VMEM((128, R), BF), pltpu.VMEM((2, 128, R), BF),
            pltpu.VMEM((2, R, 128), F32), pltpu.VMEM((2, R, 128), F32),
            pltpu.VMEM((2, R, BLK), F32), pltpu.VMEM((2, R, BLK), BF),
        ],
        compiler_params=PARAMS,
        name="attend",
    )(kept, q0t, k0, v0, q1t, k1, v1, far1, q2t, kv2_all, do0, do1, do2)
    back = lax.ppermute(back, "ctx", swap)
    back2 = lax.all_to_all(back2, "ctx", 0, 0)
    layer_p, tokens_p, gw = pl.pallas_call(
        finish,
        out_shape=[shape(R, D), shape(R, D), shape(D, 4 * D)],
        in_specs=[V] * 18,
        out_specs=[V] * 3,
        scratch_shapes=[pltpu.VMEM((R, D), BF), pltpu.VMEM((R, 384), BF), pltpu.VMEM((2, 128, 384), BF)],
        compiler_params=PARAMS,
        name="finish",
    )(xp, gp, nmt, gain2, w, wp, wo, o0, o1, o2, dq0, dq1, dq2, dk0, dv0, near, back, back2)
    gw = lax.psum(gw, ("dp", "ctx"))
    layer, grad_tokens, g_qkv, g_proj, g_gain = pl.pallas_call(
        deliver,
        out_shape=[shape(R, D), shape(R, D), shape(D, 3 * D, dtype=F32), shape(D, D, dtype=F32), shape(1, D, dtype=F32)],
        in_specs=[V] * 5,
        out_specs=[V] * 5,
        compiler_params=PARAMS,
        name="deliver",
    )(layer_p, tokens_p, gw, gain2, w)
    return layer[None], grad_tokens[None], g_qkv, g_proj, g_gain[0]


def solution(mesh):
    in_specs = (P("dp", "ctx", None), P("dp"), P(), P(), P(), P("dp", "ctx", None))
    out_specs = (P("dp", "ctx", None), P("dp", "ctx", None), P(), P(), P())
    return jax.shard_map(shards, mesh=mesh, in_specs=in_specs, out_specs=out_specs, check_vma=False)
```

```python
import functools

import jax
import jax.numpy as jnp
import numpy as np
from jax import lax
from jax.experimental import pallas as pl
from jax.experimental.pallas import tpu as pltpu
from jax.sharding import PartitionSpec as P

BF = jnp.bfloat16
F32 = jnp.float32
LOG2E = 1.4426950408889634
Q_SCALE = 0.125 * LOG2E
NEG = -1e9
R = 1024
D = 768
BLK = 256
VMEM = 60 * 1024 * 1024


def nn(a, b):
    return lax.dot_general(a, b, (((1,), (0,)), ((), ())), preferred_element_type=F32)


def nt(a, b):
    return lax.dot_general(a, b, (((1,), (1,)), ((), ())), preferred_element_type=F32)


def iota(shape, dim):
    return lax.broadcasted_iota(jnp.int32, shape, dim)


def residue(i):
    return jnp.where(i < 8, 2 * i, 2 * i - 15)


def place(p):
    return 16 * (p & 63) + residue(p >> 6)


def row_order():
    r, c = iota((256, 256), 0), iota((256, 256), 1)
    return jnp.where(c == 16 * (r & 15) + residue(r >> 4), 1.0, 0.0).astype(BF)


def row_order_back():
    c, r = iota((256, 256), 0), iota((256, 256), 1)
    return jnp.where(c == 16 * (r & 15) + residue(r >> 4), 1.0, 0.0).astype(BF)


def head_order():
    r, c = iota((256, 256), 0), iota((256, 256), 1)
    b = c >> 6
    b = jnp.where(b == 1, 2, jnp.where(b == 2, 1, b))
    return jnp.where(r == 64 * b + (c & 63), 1.0, 0.0).astype(BF)


HEAD_BLOCKS = (0, 2, 1, 3)


def split_diag(x):
    left = iota((64, 128), 1) < 64
    return jnp.where(left, x[:64], x[64:])


def diag_mask(x):
    r, c = iota((128, 128), 0), iota((128, 128), 1)
    return jnp.where((r < 64) == (c < 64), x, 0.0)


def prepare_pair(k, v, bias, ka, va, vat, kt):
    lane = iota((R, 128), 1)
    for h in range(2):
        mine = (lane < 64) == (h == 0)
        other = 64 - 64 * h
        ka[h] = jnp.where(mine, k.astype(F32), jnp.where(lane == other, bias, 0.0)).astype(BF)
        both = (lane == other) | (lane == other + 1)
        va_h = jnp.where(mine, v.astype(F32), jnp.where(both, 1.0, 0.0))
        va[h] = va_h.astype(BF)
        vat[h] = jnp.transpose(va_h).astype(BF)
    kt[...] = jnp.transpose(k.astype(F32)).astype(BF)


def prepare_queries(qt, qa):
    sub = iota(qt.shape, 0)
    for h in range(2):
        mine = (sub < 64) == (h == 0)
        other = 64 - 64 * h
        qa[h, :, : qt.shape[1]] = jnp.where(mine, qt.astype(F32), jnp.where(sub == other, 1.0, 0.0)).astype(BF)


def attend_block(h, first, cols, ok, qa, dot_, ka, va, vat, kt, dk, dv, s_ref, p_ref):
    head = slice(64 * h, 64 * h + 64)
    other = 64 - 64 * h
    q = qa[h, :, cols]
    top = None
    for c in range(4):
        keys = slice(256 * c, 256 * c + 256)
        s = nn(ka[h, keys], q)
        s_ref[h, keys] = s
        m = jnp.max(s, 0, keepdims=True)
        top = m if top is None else jnp.maximum(top, m)
    o = None
    for c in range(4):
        keys = slice(256 * c, 256 * c + 256)
        p = jnp.exp2(s_ref[h, keys] - top).astype(BF)
        p_ref[h, keys] = p
        part = nn(vat[h, :, keys], p)
        o = part if o is None else o + part
    scale = 1.0 / o[other : other + 1]
    out = jnp.where(ok, o[head] * scale, 0.0).astype(BF)
    do = dot_.astype(F32)
    inner = jnp.sum(do * out.astype(F32), 0, keepdims=True) * scale
    high = inner.astype(BF).astype(F32)
    low = inner - high
    sub = iota((64, BLK), 0)
    extra = jnp.where(sub == 0, -high, jnp.where(sub == 1, -low, 0.0))
    parts = [do * scale, extra] if h == 0 else [extra, do * scale]
    da = jnp.concatenate(parts, 0).astype(BF)
    dq = None
    for c in range(4):
        keys = slice(256 * c, 256 * c + 256)
        dp = nn(va[h, keys], da)
        p = p_ref[h, keys]
        ds = (p.astype(F32) * dp).astype(BF)
        dv_new = nt(p, da)
        dk_new = nt(ds, q)
        if first is None:
            dv[h, keys] = dv_new
            dk[h, keys] = dk_new
        else:
            dv[h, keys] += dv_new
            dk[h, keys] += dk_new
        part = nn(kt[head, keys], ds)
        dq = part if dq is None else dq + part
    return out, (dq * 0.125).astype(BF)


def join(acc, scale):
    lane = iota((acc.shape[1], 128), 1)
    return jnp.where(lane < 64, acc[0], acc[1]) * scale


def attend_pair(qt, dot_, k, v, bias, limit, start, width, outs, dqs, scr, between=None):
    ka, va, vat, kt, qa, dk, dv, s_ref, p_ref = scr
    prepare_pair(k, v, bias, ka, va, vat, kt)
    prepare_queries(qt[...], qa)
    dk[...] = jnp.zeros_like(dk)
    dv[...] = jnp.zeros_like(dv)

    def step(i, _):
        cols = pl.ds(pl.multiple_of(i * BLK, BLK), BLK)
        ok = place(iota((1, BLK), 1) + start + i * BLK) < limit
        for h in range(2):
            head = slice(64 * h, 64 * h + 64)
            o, dq = attend_block(h, i, cols, ok, qa, dot_[head, cols], ka, va, vat, kt, dk, dv, s_ref, p_ref)
            outs[head, cols] = o
            dqs[head, cols] = dq
        return 0

    if between is None:
        lax.fori_loop(0, width // BLK, step, 0)
    else:
        for i in range(width // BLK):
            lax.fori_loop(i, i + 1, step, 0)
            if between:
                between.pop(0)()


def attend_few(qd, do, k, v, bias, ok):
    s = nn(k, qd) + bias
    top = jnp.max(s, 0, keepdims=True)
    p = jnp.exp2(s - top).astype(BF)
    pf = p.astype(F32)
    scale = 1.0 / jnp.sum(pf, 0, keepdims=True)
    o = nn(jnp.transpose(v.astype(F32)).astype(BF), p) * scale
    o = jnp.where(ok, diag_mask(o), 0.0).astype(BF)
    do32 = do.astype(F32)
    inner = jnp.sum(do32 * o.astype(F32), 0, keepdims=True) * scale
    da = (do32 * scale).astype(BF)
    ds = (pf * (nn(v, da) - inner)).astype(BF)
    dq = diag_mask(nn(jnp.transpose(k.astype(F32)).astype(BF), ds)) * 0.125
    return o, dq.astype(BF), nt(ds, qd) * (1.0 / LOG2E), nt(p, da)


MESH = pl.DeviceIdType.MESH
CHUNK = 6144
HALF, PART, QUART, SMALL = 3072, 1024, 256, 64


def spread(x):
    return diag_mask(jnp.concatenate([x, x], 0))


def flip(x):
    return jnp.transpose(x.astype(F32)).astype(BF)


class Links:
    def __init__(self):
        self.dp, self.ctx = lax.axis_index("dp"), lax.axis_index("ctx")
        self.core = self.dp & 1
        y, x, z = self.dp >> 1, self.ctx >> 2, self.ctx & 3

        def low(i):
            return (i ^ (i >> 1)) & 1

        self.groups = (
            (((0, 4), (6, 0)), 2 * low(x) + (y >> 1)),
            (((2, 0), (0, 3)), 2 * low(y) + (z >> 1)),
            (((0, 1), (0, 12)), 2 * low(z) + (x >> 1)),
        )

    def peer(self, group, k):
        (a, b), _ = self.groups[group]
        dp = (a[0] if k & 2 else 0) ^ (b[0] if k & 1 else 0)
        ctx = (a[1] if k & 2 else 0) ^ (b[1] if k & 1 else 0)
        return dp, ctx

    def at(self, flips):
        return (self.dp ^ flips[0], self.ctx ^ flips[1])

    def all_flips(self):
        found = {(0, k) for k in range(1, 16)} | {(1, 0)}
        for group in range(3):
            found |= {self.peer(group, k) for k in (1, 2, 3)}
        return sorted(found)


class Reduce:
    def __init__(self, links, c, gw, red, rc, r1, a1, r2, a2, r3, send, recv):
        self.links, self.c, self.gw, self.red = links, c, gw, red
        self.rc, self.r1, self.a1, self.r2, self.a2, self.r3 = (b.at[c] for b in (rc, r1, a1, r2, a2, r3))
        self.send, self.recv = send.at[c], recv.at[c]
        self.sent = []
        self.mine = CHUNK * c + links.core * HALF

    def copy(self, src, dst, sem, flips):
        copy = pltpu.make_async_remote_copy(
            src_ref=src, dst_ref=dst, send_sem=self.send.at[sem], recv_sem=self.recv.at[sem],
            device_id=self.links.at(flips), device_id_type=MESH,
        )
        copy.start()
        self.sent.append(copy)
        return copy

    def rows(self, start, size, step=16):
        return pl.ds(pl.multiple_of(start, step), size)

    def group(self, stage, part):
        g = (part + stage) % 3
        return g, self.links.groups[g][1]

    def swap(self):
        other = self.rows(CHUNK * self.c + (1 - self.links.core) * HALF, HALF)
        self.waiting = [self.copy(self.gw.at[other], self.rc, 0, (1, 0))]

    def arrive(self):
        for copy in self.waiting:
            copy.wait_recv()

    def scatter1(self):
        self.arrive()

        def add(i, _):
            to = self.rows(self.mine + i * 512, 512)
            fr = self.rows(i * 512, 512)
            self.gw[to] = (self.gw[to].astype(F32) + self.rc[fr].astype(F32)).astype(BF)
            return 0

        lax.fori_loop(0, HALF // 512, add, 0)
        self.waiting = []
        for part in range(3):
            g, i = self.group(0, part)
            for k in (1, 2, 3):
                src = self.gw.at[self.rows(self.mine + part * PART + (i ^ k) * QUART, QUART)]
                self.waiting.append(self.copy(src, self.r1.at[part, k - 1], 1 + 3 * part + k - 1, self.links.peer(g, k)))

    def scatter2(self):
        self.arrive()
        self.waiting = []
        for part in range(3):
            _, i = self.group(0, part)
            total = self.gw[self.rows(self.mine + part * PART + i * QUART, QUART)].astype(F32)
            for k in range(3):
                total += self.r1[part, k].astype(F32)
            self.a1[part] = total.astype(BF)
            g, i = self.group(1, part)
            for k in (1, 2, 3):
                src = self.a1.at[part, self.rows((i ^ k) * SMALL, SMALL)]
                self.waiting.append(self.copy(src, self.r2.at[part, k - 1], 10 + 3 * part + k - 1, self.links.peer(g, k)))

    def share(self):
        self.arrive()
        self.waiting = []
        for part in range(3):
            _, i = self.group(1, part)
            total = self.a1[part, self.rows(i * SMALL, SMALL)].astype(F32)
            for k in range(3):
                total += self.r2[part, k].astype(F32)
            g, i = self.group(2, part)
            self.r3[part, i] = total.astype(BF)
            for k in (1, 2, 3):
                mine = self.r3.at[part, i]
                self.waiting.append(self.copy(mine, mine, 19 + 3 * part + k - 1, self.links.peer(g, k)))

    def gather2(self):
        self.arrive()
        self.waiting = []
        for part in range(3):
            total = self.r3[part, 0].astype(F32)
            for k in (1, 2, 3):
                total += self.r3[part, k].astype(F32)
            g, i2 = self.group(1, part)
            at = self.rows(self.mine + part * PART + self.group(0, part)[1] * QUART + i2 * SMALL, SMALL)
            self.red[at] = total.astype(BF)
            for k in (1, 2, 3):
                self.waiting.append(self.copy(self.red.at[at], self.red.at[at], 28 + 3 * part + k - 1, self.links.peer(g, k)))

    def gather1(self):
        self.arrive()
        self.waiting = []
        for part in range(3):
            g, i = self.group(0, part)
            at = self.rows(self.mine + part * PART + i * QUART, QUART)
            for k in (1, 2, 3):
                self.waiting.append(self.copy(self.red.at[at], self.red.at[at], 37 + 3 * part + k - 1, self.links.peer(g, k)))

    def swap_back(self):
        self.arrive()
        at = self.rows(self.mine, HALF)
        self.waiting = [self.copy(self.red.at[at], self.red.at[at], 46, (1, 0))]

    def done(self):
        self.arrive()
        for copy in self.sent:
            copy.wait_send()

    def stages(self):
        return [self.swap, self.scatter1, self.scatter2, self.share, self.gather2, self.gather1, self.swap_back]


REDUCE_SEMS = 47


def layer_kernel(
    kept, gain, tokens_hbm, grad_hbm, w_hbm, w_out_hbm,
    layer_hbm, gt_hbm, red_hbm,
    tokens, grad_out, w, w_out, xp, gp, nm, nmt, wp, wo,
    q0t, k0, v0, do0, q1t, kv1, far1, do1, q2t, kv2, do2,
    o0, o1, o2, dq0, dq1, dq2, g0, g1, g2, near, back, back_r, back2, back2_r,
    ka, va, vat, kt, qa, dk, dv, s_ref, p_ref,
    gw, red, rc, r1, a1, r2, a2, r3,
    load_sem, store_sem, send1, recv1, send2, recv2, red_send, red_recv,
):
    links = Links()
    me = links.ctx
    limit = kept[0] - me * R
    far_limit = kept[0] - (me ^ 1) * R
    barrier = pltpu.get_barrier_semaphore()
    flips = links.all_flips()
    for f in flips:
        pl.semaphore_signal(barrier, inc=1, device_id=links.at(f), device_id_type=MESH)
    loads = [
        pltpu.make_async_copy(src, dst, load_sem.at[i])
        for i, (src, dst) in enumerate(((tokens_hbm, tokens), (w_hbm, w), (grad_hbm, grad_out), (w_out_hbm, w_out)))
    ]
    for load in loads:
        load.start()
    sent = []

    def push(src, dst, send, recv, flips):
        copy = pltpu.make_async_remote_copy(
            src_ref=src, dst_ref=dst, send_sem=send, recv_sem=recv, device_id=links.at(flips), device_id_type=MESH
        )
        copy.start()
        sent.append(copy)
        return copy

    order = row_order()
    loads[0].wait()
    for t in range(4):
        x = nn(order, tokens[256 * t : 256 * t + 256])
        mean = jnp.mean(x, -1, keepdims=True)
        cent = x - mean
        inv = lax.rsqrt(jnp.mean(cent * cent, -1, keepdims=True) + 1e-05)
        n = (cent * inv * gain[...]).astype(BF)
        xb = x.astype(BF)
        for i in range(16):
            to = slice(64 * i + 16 * t, 64 * i + 16 * t + 16)
            xp[to] = xb[16 * i : 16 * i + 16]
            nm[to] = n[16 * i : 16 * i + 16]
    heads = head_order()

    def lanes(level, kind, half):
        at = (level - 1) * D + kind * 256 + 128 * half
        return slice(at, at + 128)

    loads[1].wait()
    for level in (1, 2):
        for kind in range(3):
            at = kind * D + level * 256
            wp[:, (level - 1) * D + kind * 256 : (level - 1) * D + kind * 256 + 256] = nn(w[:, at : at + 256], heads).astype(BF)
    halves = [slice(0, 512), slice(512, 1024)]
    fews = [slice(0, 128), slice(512, 640)]
    for half in range(2):
        kv1[half, 0] = nn(nm[halves[half]], wp[:, lanes(1, 1, half)]).astype(BF)
        kv1[half, 1] = nn(nm[halves[half]], wp[:, lanes(1, 2, half)]).astype(BF)
        kv2[me, 2 * half] = split_diag(nn(nm[fews[half]], wp[:, lanes(2, 1, half)])).astype(BF)
        kv2[me, 2 * half + 1] = split_diag(nn(nm[fews[half]], wp[:, lanes(2, 2, half)])).astype(BF)
    pl.semaphore_wait(barrier, len(flips))
    got1 = [push(kv1.at[half], far1.at[half], send1.at[half], recv1.at[half], (0, 1)) for half in range(2)]
    got2 = [push(kv2.at[me], kv2.at[me], send2.at[0, k - 1], recv2.at[0, k - 1], (0, k)) for k in range(1, 16)]

    loads[2].wait()
    for t in range(4):
        gb = nn(order, grad_out[256 * t : 256 * t + 256]).astype(BF)
        for i in range(16):
            gp[64 * i + 16 * t : 64 * i + 16 * t + 16] = gb[16 * i : 16 * i + 16]
    loads[3].wait()
    wo[:256] = w_out[:256]
    for level in (1, 2):
        for at, block in enumerate(HEAD_BLOCKS):
            wo[256 * level + 64 * at : 256 * level + 64 * at + 64] = w_out[256 * level + 64 * block : 256 * level + 64 * block + 64]
    for t in range(4):
        rows = slice(256 * t, 256 * t + 256)
        q0t[:, rows] = jnp.transpose(nn(nm[rows], w[:, :256]) * Q_SCALE).astype(BF)
        k0[rows] = nn(nm[rows], w[:, D : D + 256]).astype(BF)
        v0[rows] = nn(nm[rows], w[:, 2 * D : 2 * D + 256]).astype(BF)
        ok = place(iota((1, 256), 1) + 256 * t) < limit
        do0[:, rows] = jnp.where(ok, nt(wo[:256], gp[rows]), 0.0).astype(BF)
        nmt[:, rows] = jnp.transpose(nm[rows])
    for half in range(2):
        q1t[half] = jnp.transpose(nn(nm[halves[half]], wp[:, lanes(1, 0, half)]) * Q_SCALE).astype(BF)
        q2t[half] = jnp.transpose(diag_mask(nn(nm[fews[half]], wp[:, lanes(2, 0, half)])) * Q_SCALE).astype(BF)
        ok = place(iota((1, 512), 1) + 512 * half) < limit
        do1[half] = jnp.where(ok, nt(wo[256 + 128 * half : 384 + 128 * half], gp[halves[half]]), 0.0).astype(BF)
        ok = place(iota((1, 128), 1) + 512 * half) < limit
        do2[half] = jnp.where(ok, diag_mask(nt(wo[512 + 128 * half : 640 + 128 * half], gp[fews[half]])), 0.0).astype(BF)

    reduces = [Reduce(links, c, gw, red, rc, r1, a1, r2, a2, r3, red_send, red_recv) for c in range(3)]
    steps = [r.stages() for r in reduces]

    scr = (ka, va, vat, kt, qa, dk, dv, s_ref, p_ref)
    sub = iota((R, 128), 0)
    lane = iota((R, 128), 1)
    bias = jnp.where(place(sub) < limit, 0.0, NEG)
    for pair in range(2):
        c = slice(128 * pair, 128 * pair + 128)
        attend_pair(q0t.at[c], do0.at[c], k0[:, c], v0[:, c], bias, limit, 0, R, o0.at[c], dq0.at[c], scr)
        g0[:, 256 + 128 * pair : 384 + 128 * pair] = join(dk, 1.0 / LOG2E).astype(BF)
        g0[:, 512 + 128 * pair : 640 + 128 * pair] = join(dv, 1.0).astype(BF)
    for t in range(4):
        rows = slice(256 * t, 256 * t + 256)
        g0[rows, :256] = flip(dq0[:, rows])
    for kind in range(3):
        x = nn(nmt[...], g0[:, 256 * kind : 256 * kind + 256]).astype(BF)
        gw[1536 * kind : 1536 * kind + 768] = x[:, :128]
        gw[1536 * kind + 768 : 1536 * kind + 1536] = x[:, 128:]
    x = nn(o0[...], gp[...]).astype(BF)
    for t in range(6):
        gw[4608 + 256 * t : 4864 + 256 * t] = x[:, 128 * t : 128 * t + 128]
    steps[0].pop(0)()

    for copy in got2:
        copy.wait_recv()
    for half in range(2):
        at = R * (sub >> 6) + 16 * (sub & 63) + jnp.where(lane < 64, half, half + 2)
        bias = jnp.where(at < kept[0], 0.0, NEG)
        ok = place(iota((1, 128), 1) + 512 * half) < limit
        k = kv2[:, 2 * half].reshape(R, 128)
        v = kv2[:, 2 * half + 1].reshape(R, 128)
        o, dq, gk, gv = attend_few(q2t[half], do2[half], k, v, bias, ok)
        o2[half] = o
        dq2[half] = dq
        back2[:, 2 * half] = gk.astype(BF).reshape(16, 64, 128)
        back2[:, 2 * half + 1] = gv.astype(BF).reshape(16, 64, 128)
    back2_r[me] = back2[me]
    got_back2 = [
        push(back2.at[me ^ k], back2_r.at[me], send2.at[1, k - 1], recv2.at[1, k - 1], (0, k)) for k in range(1, 16)
    ]
    steps[0].pop(0)()

    got_back1 = []
    for half in range(2):
        rows = halves[half]
        at = place((sub & 511) + 512 * half)
        bias = jnp.where(at < jnp.where(sub < 512, limit, far_limit), 0.0, NEG)
        got1[half].wait_recv()
        k = jnp.concatenate([kv1[half, 0], far1[half, 0]], 0)
        v = jnp.concatenate([kv1[half, 1], far1[half, 1]], 0)
        attend_pair(
            q1t.at[half], do1.at[half], k, v, bias, limit, 512 * half, 512, o1.at[half], dq1.at[half], scr,
            between=steps[0],
        )
        gk = join(dk, 1.0 / LOG2E)
        gv = join(dv, 1.0)
        near[half, 0] = gk[:512]
        near[half, 1] = gv[:512]
        back[half, 0] = gk[512:].astype(BF)
        back[half, 1] = gv[512:].astype(BF)
        got_back1.append(push(back.at[half], back_r.at[half], send1.at[2 + half], recv1.at[2 + half], (0, 1)))

    for copy in got_back2:
        copy.wait_recv()
    for half in range(2):
        g2[half, :, :128] = flip(dq2[half])
        for kind in range(2):
            total = jnp.sum(back2_r[:, 2 * half + kind].astype(F32), 0)
            g2[half, :, 128 + 128 * kind : 256 + 128 * kind] = spread(total).astype(BF)
        x = nn(nmt[:, fews[half]], g2[half]).astype(BF)
        for kind in range(3):
            at = 2 * CHUNK + 1536 * kind + 768 * half
            gw[at : at + 768] = x[:, 128 * kind : 128 * kind + 128]
        x = nn(o2[half], gp[fews[half]]).astype(BF)
        for t in range(6):
            at = 2 * CHUNK + 4608 + 256 * t + 128 * half
            gw[at : at + 128] = x[:, 128 * t : 128 * t + 128]
    steps[2].pop(0)()
    if steps[0]:
        steps[0].pop(0)()
    for half in range(2):
        got_back1[half].wait_recv()
        g1[halves[half], :128] = flip(dq1[half])
        for kind in range(2):
            total = near[half, kind] + back_r[half, kind].astype(F32)
            g1[halves[half], 128 + 128 * kind : 256 + 128 * kind] = total.astype(BF)
        x = nn(nmt[:, halves[half]], g1[halves[half]]).astype(BF)
        for kind in range(3):
            at = CHUNK + 1536 * kind + 768 * half
            gw[at : at + 768] = x[:, 128 * kind : 128 * kind + 128]
        x = nn(o1[half], gp[halves[half]]).astype(BF)
        for t in range(6):
            at = CHUNK + 4608 + 256 * t + 128 * half
            gw[at : at + 128] = x[:, 128 * t : 128 * t + 128]
    steps[1].pop(0)()
    steps[2].pop(0)()

    for t in range(8):
        rows = slice(128 * t, 128 * t + 128)
        half = t // 4
        at = slice(128 * (t % 4), 128 * (t % 4) + 128)
        u = nt(g0[rows, :256], w[:, :256]) + nt(g0[rows, 256:512], w[:, D : D + 256]) + nt(g0[rows, 512:768], w[:, 2 * D : 2 * D + 256])
        y = nn(flip(o0[:, rows]), wo[:256]) + nn(flip(o1[half, :, at]), wo[256 + 128 * half : 384 + 128 * half])
        for kind in range(3):
            u += nt(g1[rows, 128 * kind : 128 * kind + 128], wp[:, lanes(1, kind, half)])
        if t % 4 == 0:
            for kind in range(3):
                u += nt(g2[half, :, 128 * kind : 128 * kind + 128], wp[:, lanes(2, kind, half)])
            y += nn(flip(o2[half]), wo[512 + 128 * half : 640 + 128 * half])
        x = xp[rows].astype(F32)
        tokens[rows] = (x + y).astype(BF)
        u = u * gain[...]
        cent = x - jnp.mean(x, -1, keepdims=True)
        inv = lax.rsqrt(jnp.mean(cent * cent, -1, keepdims=True) + 1e-05)
        xhat = cent * inv
        mean = jnp.mean(u, -1, keepdims=True)
        dotted = jnp.mean(u * xhat, -1, keepdims=True)
        grad_out[rows] = (gp[rows].astype(F32) + inv * (u - mean - xhat * dotted)).astype(BF)
        for c in (0, 2, 1):
            if steps[c] and (c == 0 or t % 2 == c % 2):
                steps[c].pop(0)()
    stores = [
        pltpu.make_async_copy(tokens, layer_hbm, store_sem.at[0]),
        pltpu.make_async_copy(grad_out, gt_hbm, store_sem.at[1]),
    ]
    for store in stores:
        store.start()
    while any(steps):
        for c in (0, 2, 1):
            if steps[c]:
                steps[c].pop(0)()
    for i, c in enumerate((0, 2, 1)):
        reduces[c].done()
        rows = slice(CHUNK * c, CHUNK * c + CHUNK)
        stores.append(pltpu.make_async_copy(red.at[rows], red_hbm.at[rows], store_sem.at[2 + i]))
        stores[-1].start()
    for copy in sent:
        copy.wait_send()
    for store in stores:
        store.wait()


def deliver(layer_p, tokens_p, gw, gain, w, layer, grad_tokens, g_qkv, g_proj, g_gain):
    order = row_order_back()
    for t in range(4):
        rows = slice(256 * t, 256 * t + 256)
        for src, dst in ((layer_p, layer), (tokens_p, grad_tokens)):
            x = jnp.concatenate([src[64 * i + 16 * t : 64 * i + 16 * t + 16] for i in range(16)], 0)
            dst[rows] = nn(order, x).astype(BF)
    heads = head_order()
    total = jnp.zeros((D, 128), F32)
    for level in range(3):
        for kind in range(3):
            at = CHUNK * level + 1536 * kind
            x = jnp.concatenate([gw[at : at + 768], gw[at + 768 : at + 1536]], 1)
            x = x.astype(F32) if level == 0 else nn(x, heads)
            c = slice(D * kind + 256 * level, D * kind + 256 * level + 256)
            g_qkv[:, c] = x
            prod = x * w[:, c].astype(F32)
            total += prod[:, :128] + prod[:, 128:]
        for t in range(6):
            at = CHUNK * level + 4608 + 256 * t
            for i, block in enumerate((0, 1, 2, 3) if level == 0 else HEAD_BLOCKS):
                to = 256 * level + 64 * block
                g_proj[to : to + 64, 128 * t : 128 * t + 128] = gw[at + 64 * i : at + 64 * i + 64].astype(F32)
    g_gain[...] = jnp.sum(jnp.transpose(total), 0, keepdims=True) / gain[...]


def shape(*dims, dtype=BF):
    return jax.ShapeDtypeStruct(dims, dtype)


V = pl.BlockSpec(memory_space=pltpu.VMEM)
S = pl.BlockSpec(memory_space=pltpu.SMEM)
A = pl.BlockSpec(memory_space=pl.ANY)


def vmem(*dims, dtype=BF):
    return pltpu.VMEM(dims, dtype)


def shards(tokens, kept, gain, w, w_out, grad_out):
    gain2 = gain[None]
    dma = pltpu.SemaphoreType.DMA
    layer_p, tokens_p, gw = pl.pallas_call(
        layer_kernel,
        out_shape=[shape(R, D), shape(R, D), shape(3 * CHUNK, 128)],
        in_specs=[S, V] + [A] * 4,
        out_specs=[A] * 3,
        scratch_shapes=[
            vmem(R, D), vmem(R, D), vmem(D, 3 * D), vmem(D, D), vmem(R, D), vmem(R, D), vmem(R, D), vmem(D, R),
            vmem(D, 2 * D), vmem(D, D),
            vmem(256, R), vmem(R, 256), vmem(R, 256), vmem(256, R),
            vmem(2, 128, 512), vmem(2, 2, 512, 128), vmem(2, 2, 512, 128), vmem(2, 128, 512),
            vmem(2, 128, 128), vmem(16, 4, 64, 128), vmem(2, 128, 128),
            vmem(256, R), vmem(2, 128, 512), vmem(2, 128, 128),
            vmem(256, R), vmem(2, 128, 512), vmem(2, 128, 128),
            vmem(R, D), vmem(R, 384), vmem(2, 128, 384),
            vmem(2, 2, 512, 128, dtype=F32), vmem(2, 2, 512, 128), vmem(2, 2, 512, 128),
            vmem(16, 4, 64, 128), vmem(16, 4, 64, 128),
            vmem(2, R, 128), vmem(2, R, 128), vmem(2, 128, R), vmem(128, R), vmem(2, 128, R),
            vmem(2, R, 128, dtype=F32), vmem(2, R, 128, dtype=F32),
            vmem(2, R, BLK, dtype=F32), vmem(2, R, BLK),
            vmem(3 * CHUNK, 128), vmem(3 * CHUNK, 128), vmem(3, HALF, 128),
            vmem(3, 3, 3, QUART, 128), vmem(3, 3, QUART, 128), vmem(3, 3, 3, SMALL, 128), vmem(3, 3, SMALL, 128),
            vmem(3, 3, 4, SMALL, 128),
            dma((4,)), dma((5,)), dma((4,)), dma((4,)), dma((2, 15)), dma((2, 15)),
            dma((3, REDUCE_SEMS)), dma((3, REDUCE_SEMS)),
        ],
        compiler_params=pltpu.CompilerParams(vmem_limit_bytes=VMEM, collective_id=0, has_side_effects=True),
        name="layer",
    )(kept, gain2, tokens[0], grad_out[0], w, w_out)
    layer, grad_tokens, g_qkv, g_proj, g_gain = pl.pallas_call(
        deliver,
        out_shape=[shape(R, D), shape(R, D), shape(D, 3 * D, dtype=F32), shape(D, D, dtype=F32), shape(1, D, dtype=F32)],
        in_specs=[V] * 5,
        out_specs=[V] * 5,
        compiler_params=pltpu.CompilerParams(vmem_limit_bytes=VMEM),
        name="deliver",
    )(layer_p, tokens_p, gw, gain2, w)
    return layer[None], grad_tokens[None], g_qkv, g_proj, g_gain[0]


def solution(mesh):
    in_specs = (P("dp", "ctx", None), P("dp"), P(), P(), P(), P("dp", "ctx", None))
    out_specs = (P("dp", "ctx", None), P("dp", "ctx", None), P(), P(), P())
    return jax.shard_map(shards, mesh=mesh, in_specs=in_specs, out_specs=out_specs, check_vma=False)
```

```python
import functools

import jax
import jax.numpy as jnp
import numpy as np
from jax import lax
from jax.experimental import pallas as pl
from jax.experimental.pallas import tpu as pltpu
from jax.sharding import PartitionSpec as P

BF = jnp.bfloat16
F32 = jnp.float32
LOG2E = 1.4426950408889634
Q_SCALE = 0.125 * LOG2E
NEG = -1e9
R = 1024
D = 768
BLK = 512
FEW = 256
VMEM = 60 * 1024 * 1024


def nn(a, b):
    return lax.dot_general(a, b, (((1,), (0,)), ((), ())), preferred_element_type=F32)


def nt(a, b):
    return lax.dot_general(a, b, (((1,), (1,)), ((), ())), preferred_element_type=F32)


def iota(shape, dim):
    return lax.broadcasted_iota(jnp.int32, shape, dim)


def residue(i):
    return jnp.where(i < 8, 2 * i, 2 * i - 15)


def place(p):
    return 16 * (p & 63) + residue(p >> 6)


def row_order():
    r, c = iota((256, 256), 0), iota((256, 256), 1)
    return jnp.where(c == 16 * (r & 15) + residue(r >> 4), 1.0, 0.0).astype(BF)


def row_order_back():
    c, r = iota((256, 256), 0), iota((256, 256), 1)
    return jnp.where(c == 16 * (r & 15) + residue(r >> 4), 1.0, 0.0).astype(BF)


def head_order():
    r, c = iota((256, 256), 0), iota((256, 256), 1)
    b = c >> 6
    b = jnp.where(b == 1, 2, jnp.where(b == 2, 1, b))
    return jnp.where(r == 64 * b + (c & 63), 1.0, 0.0).astype(BF)


HEAD_BLOCKS = (0, 2, 1, 3)


def diag_mask(x):
    r, c = iota((128, 128), 0), iota((128, 128), 1)
    return jnp.where((r < 64) == (c < 64), x, 0.0)


MESH = pl.DeviceIdType.MESH


def flip(x):
    return jnp.transpose(x.astype(F32)).astype(BF)


def half_turn(x):
    return pltpu.roll(x, 64, 1)


class Links:
    def __init__(self):
        self.dp, self.ctx = lax.axis_index("dp"), lax.axis_index("ctx")
        self.core = self.dp & 1
        self.y, self.x, self.z = self.dp >> 1, self.ctx >> 2, self.ctx & 3

        def low(i):
            return (i ^ (i >> 1)) & 1

        self.groups = (
            (((0, 4), (6, 0)), 2 * low(self.x) + (self.y >> 1)),
            (((2, 0), (0, 3)), 2 * low(self.y) + (self.z >> 1)),
            (((0, 1), (0, 12)), 2 * low(self.z) + (self.x >> 1)),
        )

    def peer(self, group, k):
        (a, b), _ = self.groups[group]
        dp = (a[0] if k & 2 else 0) ^ (b[0] if k & 1 else 0)
        ctx = (a[1] if k & 2 else 0) ^ (b[1] if k & 1 else 0)
        return dp, ctx

    def at(self, flips):
        return (self.dp ^ flips[0], self.ctx ^ flips[1])

    def all_flips(self):
        found = {(1, 0)}
        for k in (1, 2, 3):
            found |= {(0, k), (0, 4 * k)}
            for group in range(3):
                found.add(self.peer(group, k))
        return sorted(found)


def at_rows(start, size):
    return pl.ds(pl.multiple_of(start, 16), size)


class Reduce:
    def __init__(self, links, c, start, size, gw, red, rc, r1, a1, r2, r3, send, recv):
        self.links, self.start, self.gw, self.red = links, start, gw, red
        self.half, self.part, self.quart, self.small = size // 2, size // 6, size // 24, size // 96
        self.rc = rc.at[pl.ds(start // 2, size // 2)]
        self.r1 = r1.at[pl.ds(start * 3 // 8, size * 3 // 8)]
        self.a1 = a1.at[pl.ds(start // 8, size // 8)]
        self.r2 = r2.at[pl.ds(start * 3 // 32, size * 3 // 32)]
        self.r3 = r3.at[pl.ds(start // 8, size // 8)]
        self.send, self.recv = send.at[c], recv.at[c]
        self.sent = []
        self.waiting = []
        self.mine = start + links.core * self.half
        self.todo = [self.swap, self.scatter1, self.scatter2, self.share, self.gather2, self.gather1, self.swap_back]

    def step(self):
        if self.todo:
            self.todo.pop(0)()

    def copy(self, src, dst, sem, flips):
        copy = pltpu.make_async_remote_copy(
            src_ref=src, dst_ref=dst, send_sem=self.send.at[sem], recv_sem=self.recv.at[sem],
            device_id=self.links.at(flips), device_id_type=MESH,
        )
        copy.start()
        self.sent.append(copy)
        self.waiting.append(copy)

    def arrive(self):
        for copy in self.waiting:
            copy.wait_recv()
        self.waiting = []

    def group(self, stage, part):
        g = (part + stage) % 3
        return g, self.links.groups[g][1]

    def swap(self):
        other = at_rows(self.start + (1 - self.links.core) * self.half, self.half)
        self.copy(self.gw.at[other], self.rc, 0, (1, 0))

    def scatter1(self):
        self.arrive()

        def add(i, _):
            to = at_rows(self.mine + i * 512, 512)
            fr = at_rows(i * 512, 512)
            self.gw[to] = (self.gw[to].astype(F32) + self.rc[fr].astype(F32)).astype(BF)
            return 0

        lax.fori_loop(0, self.half // 512, add, 0)
        for part in range(3):
            g, i = self.group(0, part)
            for k in (1, 2, 3):
                src = self.gw.at[at_rows(self.mine + part * self.part + (i ^ k) * self.quart, self.quart)]
                at = 3 * part + k - 1
                self.copy(src, self.r1.at[pl.ds(at * self.quart, self.quart)], 1 + at, self.links.peer(g, k))

    def scatter2(self):
        self.arrive()
        for part in range(3):
            _, i = self.group(0, part)
            total = self.gw[at_rows(self.mine + part * self.part + i * self.quart, self.quart)].astype(F32)
            for k in range(3):
                at = (3 * part + k) * self.quart
                total += self.r1[at : at + self.quart].astype(F32)
            self.a1[part * self.quart : (part + 1) * self.quart] = total.astype(BF)
            g, i = self.group(1, part)
            for k in (1, 2, 3):
                src = self.a1.at[at_rows(part * self.quart + (i ^ k) * self.small, self.small)]
                at = 3 * part + k - 1
                self.copy(src, self.r2.at[pl.ds(at * self.small, self.small)], 10 + at, self.links.peer(g, k))

    def share(self):
        self.arrive()
        for part in range(3):
            _, i = self.group(1, part)
            total = self.a1[at_rows(part * self.quart + i * self.small, self.small)].astype(F32)
            for k in range(3):
                at = (3 * part + k) * self.small
                total += self.r2[at : at + self.small].astype(F32)
            g, i = self.group(2, part)
            here = at_rows((4 * part + i) * self.small, self.small)
            self.r3[here] = total.astype(BF)
            for k in (1, 2, 3):
                self.copy(self.r3.at[here], self.r3.at[here], 19 + 3 * part + k - 1, self.links.peer(g, k))

    def gather2(self):
        self.arrive()
        for part in range(3):
            total = None
            for k in range(4):
                at = (4 * part + k) * self.small
                x = self.r3[at : at + self.small].astype(F32)
                total = x if total is None else total + x
            g, i2 = self.group(1, part)
            at = at_rows(self.mine + part * self.part + self.group(0, part)[1] * self.quart + i2 * self.small, self.small)
            self.red[at] = total.astype(BF)
            for k in (1, 2, 3):
                self.copy(self.red.at[at], self.red.at[at], 28 + 3 * part + k - 1, self.links.peer(g, k))

    def gather1(self):
        self.arrive()
        for part in range(3):
            g, i = self.group(0, part)
            at = at_rows(self.mine + part * self.part + i * self.quart, self.quart)
            for k in (1, 2, 3):
                self.copy(self.red.at[at], self.red.at[at], 37 + 3 * part + k - 1, self.links.peer(g, k))

    def swap_back(self):
        self.arrive()
        at = at_rows(self.mine, self.half)
        self.copy(self.red.at[at], self.red.at[at], 46, (1, 0))

    def done(self):
        while self.todo:
            self.step()
        self.arrive()


REDUCE_SEMS = 47
LEVEL1, LEVEL2, PAIRS = 0, 6144, (12288, 15360)
STARTS, SIZES = (0, 12288, 15360), (12288, 3072, 3072)
GRADS = 18432


def prepare_keys(slot, kh, vh, k, v, bias, ka, va, vat):
    lane = iota((R, 128), 1)
    ka[slot] = jnp.where((lane < 64) == (kh == 0), k, jnp.where(lane == 64 - 64 * kh, bias, 0.0)).astype(BF)
    other = 64 - 64 * vh
    va_h = jnp.where((lane < 64) == (vh == 0), v, jnp.where((lane == other) | (lane == other + 1), 1.0, 0.0))
    va[slot] = va_h.astype(BF)
    vat[slot] = jnp.transpose(va_h).astype(BF)


def prepare_queries(slot, kh, qt, qa):
    sub = iota(qt.shape, 0)
    x = jnp.where((sub < 64) == (kh == 0), qt.astype(F32), jnp.where(sub == 64 - 64 * kh, 1.0, 0.0))
    qa[slot, :, : qt.shape[1]] = x.astype(BF)


class Attend:
    def __init__(self, slot, kh, vh, add, q, ok, dot_, scr):
        self.slot, self.kh, self.vh, self.add = slot, kh, vh, add
        self.q, self.ok, self.dot_ = q, ok, dot_
        self.width = q.shape[1]
        self.ka, self.va, self.vat, self.kt, _, self.dk, self.dv, self.s_ref, self.p_ref = scr
        self.top = self.o = self.dq = None

    def scores(self, keys):
        s = nn(self.ka[self.slot, keys], self.q)
        self.s_ref[self.slot, keys, : self.width] = s
        m = jnp.max(s, 0, keepdims=True)
        self.top = m if self.top is None else jnp.maximum(self.top, m)

    def mix(self, keys):
        p = jnp.exp2(self.s_ref[self.slot, keys, : self.width] - self.top).astype(BF)
        self.p_ref[self.slot, keys, : self.width] = p
        part = nn(self.vat[self.slot, :, keys], p)
        self.o = part if self.o is None else self.o + part

    def turn(self):
        other, vh = 64 - 64 * self.vh, self.vh
        scale = 1.0 / self.o[other : other + 1]
        self.out = jnp.where(self.ok, self.o[64 * vh : 64 * vh + 64] * scale, 0.0).astype(BF)
        do = self.dot_.astype(F32)
        inner = jnp.sum(do * self.out.astype(F32), 0, keepdims=True) * scale
        high = inner.astype(BF).astype(F32)
        sub = iota((64, self.width), 0)
        extra = jnp.where(sub == 0, -high, jnp.where(sub == 1, high - inner, 0.0))
        parts = [do * scale, extra] if vh == 0 else [extra, do * scale]
        self.da = jnp.concatenate(parts, 0).astype(BF)

    def back(self, keys):
        slot, kh = self.slot, self.kh
        dp = nn(self.va[slot, keys], self.da)
        p = self.p_ref[slot, keys, : self.width]
        ds = (p.astype(F32) * dp).astype(BF)
        if self.add:
            self.dv[slot, keys] += nt(p, self.da)
            self.dk[slot, keys] += nt(ds, self.q)
        else:
            self.dv[slot, keys] = nt(p, self.da)
            self.dk[slot, keys] = nt(ds, self.q)
        part = nn(self.kt[64 * kh : 64 * kh + 64, keys], ds)
        self.dq = part if self.dq is None else self.dq + part

    def results(self):
        return self.out, (self.dq * 0.125).astype(BF)


KEYS = [slice(256 * c, 256 * c + 256) for c in range(4)]


def attend_one(a):
    for keys in KEYS:
        a.scores(keys)
    for keys in KEYS:
        a.mix(keys)
    a.turn()
    for keys in KEYS:
        a.back(keys)


def attend_two(a, b):
    for keys in KEYS:
        a.scores(keys)
    for keys in KEYS:
        a.mix(keys)
        b.scores(keys)
    a.turn()
    for keys in KEYS:
        a.back(keys)
        b.mix(keys)
    b.turn()
    for keys in KEYS:
        b.back(keys)


def join(acc, scale):
    lane = iota((acc.shape[1], 128), 1)
    return jnp.where(lane < 64, acc[0], acc[1]) * scale


def attend_pair(qt, dot_, k, v, bias, limit, start, width, outs, dqs, scr, between=None):
    ka, va, vat, kt, qa, dk, dv, s_ref, p_ref = scr
    k, v = k.astype(F32), v.astype(F32)
    for h in range(2):
        prepare_keys(h, h, h, k, v, bias, ka, va, vat)
        prepare_queries(h, h, qt[...], qa)
    kt[...] = jnp.transpose(k).astype(BF)
    dk[...] = jnp.zeros_like(dk)
    dv[...] = jnp.zeros_like(dv)

    def step(i, _):
        cols = pl.ds(pl.multiple_of(i * BLK, BLK), BLK)
        ok = place(iota((1, BLK), 1) + start + i * BLK) < limit
        two = [Attend(h, h, h, True, qa[h, :, cols], ok, dot_[64 * h : 64 * h + 64, cols], scr) for h in range(2)]
        attend_two(*two)
        for h in range(2):
            outs[64 * h : 64 * h + 64, cols], dqs[64 * h : 64 * h + 64, cols] = two[h].results()
        return 0

    if between is None:
        lax.fori_loop(0, width // BLK, step, 0)
    else:
        i = 0
        for count, action in between:
            lax.fori_loop(i, i + count, step, 0)
            i += count
            if action is not None:
                action()


def blocks_of(first, second):
    first, second = first.astype(F32), second.astype(F32)
    a = diag_mask(jnp.concatenate([first, half_turn(second)], 0))
    b = diag_mask(jnp.concatenate([half_turn(first), second], 0))
    return a, b


def pack_heads(a, b):
    left = iota((64, 128), 1) < 64
    return (
        jnp.where(left, a[:64], half_turn(b[:64])),
        jnp.where(left, half_turn(a[64:]), b[64:]),
    )


def layer_kernel(
    kept, gain_ref, tokens_hbm, grad_hbm, w_hbm, w_out_hbm,
    layer_hbm, gt_hbm, red_hbm,
    tokens, grad_out, w, w_out, xp, gp, nm, nmt, wp, wo,
    q0t, k0, v0, do0, q1t, kv1, far1, do1, src2, kv2, qd2,
    o0, o1, dq0, dq1, g0, g1, g2, near, back, back_r, xb2, xr2, zb2, zr2,
    ka, va, vat, kt, qa, dk, dv, s_ref, p_ref,
    gw, red, rc, r1, a1, r2, r3, u_ref,
    load_sem, store_sem, send1, recv1, send2, recv2, red_send, red_recv,
):
    links = Links()
    me, mx, mz = links.ctx, links.x, links.z
    limit = kept[0] - me * R
    far_limit = kept[0] - (me ^ 1) * R
    gain = gain_ref[...].reshape(1, D)
    barrier = pltpu.get_barrier_semaphore()
    flips = links.all_flips()
    for f in flips:
        pl.semaphore_signal(barrier, inc=1, device_id=links.at(f), device_id_type=MESH)
    loads = [
        pltpu.make_async_copy(src, dst, load_sem.at[i])
        for i, (src, dst) in enumerate(((tokens_hbm, tokens), (w_hbm, w), (grad_hbm, grad_out), (w_out_hbm, w_out)))
    ]
    for load in loads:
        load.start()
    sent = []

    def push(src, dst, send, recv, flips):
        copy = pltpu.make_async_remote_copy(
            src_ref=src, dst_ref=dst, send_sem=send, recv_sem=recv, device_id=links.at(flips), device_id_type=MESH
        )
        copy.start()
        sent.append(copy)
        return copy

    order = row_order()
    loads[0].wait()
    for t in range(4):
        x = nn(order, tokens[256 * t : 256 * t + 256])
        mean = jnp.mean(x, -1, keepdims=True)
        cent = x - mean
        inv = lax.rsqrt(jnp.mean(cent * cent, -1, keepdims=True) + 1e-05)
        n = (cent * inv * gain).astype(BF)
        xb = x.astype(BF)
        for i in range(16):
            to = slice(64 * i + 16 * t, 64 * i + 16 * t + 16)
            xp[to] = xb[16 * i : 16 * i + 16]
            nm[to] = n[16 * i : 16 * i + 16]
    heads = head_order()
    halves = [slice(0, 512), slice(512, 1024)]
    fews = [slice(0, 128), slice(512, 640)]

    def order_columns(level, kind):
        at = kind * D + level * 256
        x = nn(w[:, at : at + 256], heads).astype(BF)
        for half in range(2):
            to = 768 * level + 384 * half + 128 * kind
            wp[:, to : to + 128] = x[:, 128 * half : 128 * half + 128]

    loads[1].wait()
    for kind in (1, 2):
        order_columns(1, kind)
    for half in range(2):
        at = 768 + 384 * half
        x = nn(nm[halves[half]], wp[:, at + 128 : at + 384]).astype(BF)
        kv1[half, 0] = x[:, :128]
        kv1[half, 1] = x[:, 128:]
    pl.semaphore_wait(barrier, len(flips))
    got1 = [push(kv1.at[0], far1.at[0], send1.at[0], recv1.at[0], (0, 1))]

    order_columns(1, 0)
    for kind in range(3):
        order_columns(2, kind)
        for pair in range(2):
            at = D * kind + 128 * pair
            wp[:, 384 * pair + 128 * kind : 384 * pair + 128 * kind + 128] = w[:, at : at + 128]
    loads[2].wait()
    for t in range(4):
        gb = nn(order, grad_out[256 * t : 256 * t + 256]).astype(BF)
        for i in range(16):
            gp[64 * i + 16 * t : 64 * i + 16 * t + 16] = gb[16 * i : 16 * i + 16]
    loads[3].wait()
    wo[:256] = w_out[:256]
    for level in (1, 2):
        for at, block in enumerate(HEAD_BLOCKS):
            wo[256 * level + 64 * at : 256 * level + 64 * at + 64] = w_out[256 * level + 64 * block : 256 * level + 64 * block + 64]
    for half in range(2):
        at = 1536 + 384 * half
        x = nn(nm[fews[half]], wp[:, at : at + 384])
        do = nt(gp[fews[half]], wo[512 + 128 * half : 640 + 128 * half])
        do = jnp.where(place(iota((128, 128), 0) + 512 * half) < limit, do, 0.0)
        for kind, (a, b) in enumerate(((x[:, 128:256], x[:, 256:]), (x[:, :128] * Q_SCALE, do))):
            first, second = pack_heads(a, b)
            src2[half, kind] = first.astype(BF)
            src2[half + 2, kind] = second.astype(BF)
    kv2[me] = src2[mz, 0]
    qd2[mz] = src2[mz, 1]
    got2 = []
    for k in (1, 2, 3):
        got2.append(push(src2.at[mz ^ k, 0], kv2.at[me], send2.at[k], recv2.at[k], (0, k)))
        got2.append(push(src2.at[mz ^ k, 1], qd2.at[mz], send2.at[3 + k], recv2.at[3 + k], (0, k)))
    got1.append(push(kv1.at[1], far1.at[1], send1.at[1], recv1.at[1], (0, 1)))
    q = jnp.transpose(nn(nm[...], w[:, :256]) * Q_SCALE).astype(BF)
    q0t[...] = q
    k0[...] = nn(nm[...], w[:, D : D + 256]).astype(BF)
    v0[...] = nn(nm[...], w[:, 2 * D : 2 * D + 256]).astype(BF)
    ok = place(iota((1, R), 1)) < limit
    do0[...] = jnp.where(ok, nt(wo[:256], gp[...]), 0.0).astype(BF)
    nmt[...] = jnp.transpose(nm[...])
    for half in range(2):
        at = 768 + 384 * half
        q1t[half] = jnp.transpose(nn(nm[halves[half]], wp[:, at : at + 128]) * Q_SCALE).astype(BF)
        ok = place(iota((1, 512), 1) + 512 * half) < limit
        do1[half] = jnp.where(ok, nt(wo[256 + 128 * half : 384 + 128 * half], gp[halves[half]]), 0.0).astype(BF)
    plane = pl.ds(4 * mx, 4)
    got_x = []

    def level2_keys():
        for copy in got2:
            copy.wait_recv()
        for k in (1, 2, 3):
            got_x.append(push(kv2.at[plane], kv2.at[plane], send2.at[6 + k], recv2.at[6 + k], (0, 4 * k)))

    reduces = [
        Reduce(links, c, STARTS[c], SIZES[c], gw, red, rc, r1, a1, r2, r3, red_send, red_recv) for c in range(3)
    ]
    scr = (ka, va, vat, kt, qa, dk, dv, s_ref, p_ref)
    sub = iota((R, 128), 0)
    lane = iota((R, 128), 1)
    bias0 = jnp.where(place(sub) < limit, 0.0, NEG)

    def level0(pair, between):
        c = slice(128 * pair, 128 * pair + 128)
        attend_pair(q0t.at[c], do0.at[c], k0[:, c], v0[:, c], bias0, limit, 0, R, o0.at[c], dq0.at[c], scr, between)
        at = 384 * pair
        g0[:, at : at + 128] = flip(dq0[c])
        g0[:, at + 128 : at + 256] = join(dk, 1.0 / LOG2E).astype(BF)
        g0[:, at + 256 : at + 384] = join(dv, 1.0).astype(BF)
        x = nn(nmt[...], g0[:, at : at + 384]).astype(BF)
        for kind in range(3):
            to = PAIRS[pair] + 768 * kind
            gw[to : to + 768] = x[:, 128 * kind : 128 * kind + 128]
        x = nn(o0[c], gp[...]).astype(BF)
        for t in range(6):
            to = PAIRS[pair] + 2304 + 128 * t
            gw[to : to + 128] = x[:, 128 * t : 128 * t + 128]

    def level2():
        for copy in got_x:
            copy.wait_recv()
        bias = jnp.where(R * (sub >> 6) + 16 * (sub & 63) + mz < kept[0], 0.0, NEG)
        kv = kv2[...].reshape(R, 128).astype(F32)
        prepare_keys(0, 0, 1, kv, kv, bias, ka, va, vat)
        kt[...] = jnp.transpose(kv).astype(BF)
        qdt = flip(qd2[...].reshape(256, 128))
        prepare_queries(0, 0, qdt, qa)
        col = iota((1, FEW), 1)
        ok = R * (4 * mx + (col >> 6)) + 16 * (col & 63) + mz < kept[0]
        head = Attend(0, 0, 1, False, qa[0, :, :FEW], ok, qdt[64:], scr)
        attend_one(head)
        o, dq = head.results()
        zb2[:, 1] = flip(jnp.concatenate([o, dq], 0)).reshape(4, 64, 128)
        xb2[...] = jnp.where(lane < 64, dk[0] * (1.0 / LOG2E), dv[0]).astype(BF).reshape(16, 64, 128)
        got_x[:] = [
            push(xb2.at[pl.ds(4 * (mx ^ k), 4)], xr2.at[k - 1], send2.at[9 + k], recv2.at[9 + k], (0, 4 * k)) for k in (1, 2, 3)
        ]

    got_z = []

    def level2_back():
        for copy in got_x:
            copy.wait_recv()
        total = xb2[plane].astype(F32)
        for k in range(3):
            total += xr2[k].astype(F32)
        zb2[:, 0] = total.astype(BF)
        zr2[mz] = zb2[mz]
        for k in (1, 2, 3):
            got_z.append(push(zb2.at[mz ^ k], zr2.at[mz], send2.at[12 + k], recv2.at[12 + k], (0, k)))

    outs2 = []

    def level2_grads():
        for copy in got_z:
            copy.wait_recv()
        for half in range(2):
            o, dq = blocks_of(zr2[half, 1], zr2[half + 2, 1])
            outs2.append(o.astype(BF))
            gk, gv = blocks_of(zr2[half, 0], zr2[half + 2, 0])
            for kind, x in enumerate((dq, gk, gv)):
                g2[half, :, 128 * kind : 128 * kind + 128] = x.astype(BF)
            x = nn(nmt[:, fews[half]], g2[half]).astype(BF)
            for kind in range(3):
                at = LEVEL2 + 1536 * kind + 768 * half
                gw[at : at + 768] = x[:, 128 * kind : 128 * kind + 128]
            x = nn(jnp.transpose(o).astype(BF), gp[fews[half]]).astype(BF)
            for t in range(6):
                at = LEVEL2 + 4608 + 256 * t + 128 * half
                gw[at : at + 128] = x[:, 128 * t : 128 * t + 128]

    got_back1 = []

    def level1(half):
        rows = halves[half]
        at = place((sub & 511) + 512 * half)
        bias = jnp.where(at < jnp.where(sub < 512, limit, far_limit), 0.0, NEG)
        got1[half].wait_recv()
        k = jnp.concatenate([kv1[half, 0], far1[half, 0]], 0)
        v = jnp.concatenate([kv1[half, 1], far1[half, 1]], 0)
        attend_pair(q1t.at[half], do1.at[half], k, v, bias, limit, 512 * half, 512, o1.at[half], dq1.at[half], scr)
        gk = join(dk, 1.0 / LOG2E)
        gv = join(dv, 1.0)
        near[half, 0] = gk[:512]
        near[half, 1] = gv[:512]
        back[half, 0] = gk[512:].astype(BF)
        back[half, 1] = gv[512:].astype(BF)
        got_back1.append(push(back.at[half], back_r.at[half], send1.at[2 + half], recv1.at[2 + half], (0, 1)))

    def level1_grads():
        for half in range(2):
            got_back1[half].wait_recv()
            g1[halves[half], :128] = flip(dq1[half])
            for kind in range(2):
                total = near[half, kind] + back_r[half, kind].astype(F32)
                g1[halves[half], 128 + 128 * kind : 256 + 128 * kind] = total.astype(BF)
            x = nn(nmt[:, halves[half]], g1[halves[half]]).astype(BF)
            for kind in range(3):
                at = LEVEL1 + 1536 * kind + 768 * half
                gw[at : at + 768] = x[:, 128 * kind : 128 * kind + 128]
            x = nn(o1[half], gp[halves[half]]).astype(BF)
            for t in range(6):
                at = LEVEL1 + 4608 + 256 * t + 128 * half
                gw[at : at + 128] = x[:, 128 * t : 128 * t + 128]

    level1(0)
    level2_keys()
    level2()
    level1(1)

    def grads12():
        level2_grads()
        level1_grads()
        reduces[0].step()

    level2_back()
    level0(0, [(1, grads12), (1, reduces[0].step)])
    reduces[1].step()

    def gap():
        reduces[1].step()
        reduces[0].step()

    level0(1, [(1, gap), (1, reduces[1].step)])
    reduces[0].step()
    reduces[2].step()

    for half in range(2):
        rows = halves[half]
        few = fews[half]
        at = 768 + 384 * half
        u_ref[...] = nt(g0[rows], wp[:, :768])
        u_ref[...] += nt(g1[rows], wp[:, at : at + 384])
        u_ref[:128] += nt(g2[half], wp[:, 768 + at : 1152 + at])
        reduces[2].step()
        for t in range(4):
            here = slice(512 * half + 128 * t, 512 * half + 128 * t + 128)
            x = xp[here].astype(F32)
            u = u_ref[128 * t : 128 * t + 128] * gain
            cent = x - jnp.mean(x, -1, keepdims=True)
            inv = lax.rsqrt(jnp.mean(cent * cent, -1, keepdims=True) + 1e-05)
            xhat = cent * inv
            mean = jnp.mean(u, -1, keepdims=True)
            dotted = jnp.mean(u * xhat, -1, keepdims=True)
            grad_out[here] = (gp[here].astype(F32) + inv * (u - mean - xhat * dotted)).astype(BF)
            if t == 1:
                reduces[1].step()
                reduces[0].step()
        u_ref[...] = nn(flip(o0[:, rows]), wo[:256]) + nn(flip(o1[half]), wo[256 + 128 * half : 384 + 128 * half])
        u_ref[:128] += nn(outs2[half], wo[512 + 128 * half : 640 + 128 * half])
        tokens[rows] = (xp[rows].astype(F32) + u_ref[...]).astype(BF)
        reduces[1].step()
        reduces[2].step()
        reduces[0].step()
    stores = [
        pltpu.make_async_copy(tokens, layer_hbm, store_sem.at[0]),
        pltpu.make_async_copy(grad_out, gt_hbm, store_sem.at[1]),
    ]
    for store in stores:
        store.start()
    while any(r.todo for r in reduces):
        for r in reduces:
            r.step()
    for c in range(3):
        reduces[c].done()
        rows = slice(STARTS[c], STARTS[c] + SIZES[c])
        stores.append(pltpu.make_async_copy(red.at[rows], red_hbm.at[rows], store_sem.at[2 + c]))
        stores[-1].start()
        sent.extend(reduces[c].sent)
    for copy in sent:
        copy.wait_send()
    for store in stores:
        store.wait()


def deliver(
    layer_in, tokens_in, gw_in, gain, w_in, layer_out, tokens_out, qkv_out, proj_out, g_gain,
    src, gw, w, dst, qkv, proj, load_sem, store_sem,
):
    loads = [pltpu.make_async_copy(x, src.at[i], load_sem.at[i]) for i, x in enumerate((layer_in, tokens_in))]
    for i, at in enumerate((PAIRS[0], PAIRS[1], LEVEL2, LEVEL1)):
        rows = pl.ds(at, 3072 if i < 2 else 6144)
        loads.append(pltpu.make_async_copy(gw_in.at[rows], gw.at[rows], load_sem.at[2 + i]))
    loads.append(pltpu.make_async_copy(w_in, w, load_sem.at[6]))
    for load in loads:
        load.start()
    stores = []

    def store(x, y):
        stores.append(pltpu.make_async_copy(x, y, store_sem.at[len(stores)]))
        stores[-1].start()

    order = row_order_back()
    for i, out in enumerate((layer_out, tokens_out)):
        loads[i].wait()
        for t in range(4):
            x = jnp.concatenate([src[i, 64 * j + 16 * t : 64 * j + 16 * t + 16] for j in range(16)], 0)
            dst[i, 256 * t : 256 * t + 256] = nn(order, x).astype(BF)
        store(dst.at[i], out)
    heads = head_order()
    total = jnp.zeros((D, 128), F32)
    loads[6].wait()
    for level in range(3):
        if level == 0:
            loads[2].wait()
            loads[3].wait()
        else:
            loads[6 - level].wait()
        for kind in range(3):
            if level == 0:
                ats = [at + 768 * kind for at in PAIRS]
            else:
                ats = [(0, LEVEL1, LEVEL2)[level] + 1536 * kind + 768 * pair for pair in range(2)]
            x = jnp.concatenate([gw[at : at + 768] for at in ats], 1)
            x = x.astype(F32) if level == 0 else nn(x, heads)
            c = slice(D * kind + 256 * level, D * kind + 256 * level + 256)
            qkv[:, c] = x
            store(qkv.at[:, c], qkv_out.at[:, c])
            prod = x * w[:, c].astype(F32)
            total += prod[:, :128] + prod[:, 128:]
        for t in range(6):
            for i, block in enumerate((0, 1, 2, 3) if level == 0 else HEAD_BLOCKS):
                if level == 0:
                    at = PAIRS[i // 2] + 2304 + 128 * t + 64 * (i % 2)
                else:
                    at = (0, LEVEL1, LEVEL2)[level] + 4608 + 256 * t + 64 * i
                to = 256 * level + 64 * block
                proj[to : to + 64, 128 * t : 128 * t + 128] = gw[at : at + 64].astype(F32)
        rows = pl.ds(256 * level, 256)
        store(proj.at[rows], proj_out.at[rows])
    g_gain[...] = (jnp.sum(jnp.transpose(total), 0, keepdims=True) / gain[...].reshape(1, D)).reshape(D)
    for copy in stores:
        copy.wait()


def shape(*dims, dtype=BF):
    return jax.ShapeDtypeStruct(dims, dtype)


V = pl.BlockSpec(memory_space=pltpu.VMEM)
S = pl.BlockSpec(memory_space=pltpu.SMEM)
A = pl.BlockSpec(memory_space=pl.ANY)


def vmem(*dims, dtype=BF):
    return pltpu.VMEM(dims, dtype)


def shards(tokens, kept, gain, w, w_out, grad_out):
    dma = pltpu.SemaphoreType.DMA
    layer_p, tokens_p, gw = pl.pallas_call(
        layer_kernel,
        out_shape=[shape(R, D), shape(R, D), shape(GRADS, 128)],
        in_specs=[S, V] + [A] * 4,
        out_specs=[A] * 3,
        scratch_shapes=[
            vmem(R, D), vmem(R, D), vmem(D, 3 * D), vmem(D, D), vmem(R, D), vmem(R, D), vmem(R, D), vmem(D, R),
            vmem(D, 3 * D), vmem(D, D),
            vmem(256, R), vmem(R, 256), vmem(R, 256), vmem(256, R),
            vmem(2, 128, 512), vmem(2, 2, 512, 128), vmem(2, 2, 512, 128), vmem(2, 128, 512),
            vmem(4, 2, 64, 128), vmem(16, 64, 128), vmem(4, 64, 128),
            vmem(256, R), vmem(2, 128, 512), vmem(256, R), vmem(2, 128, 512),
            vmem(R, D), vmem(R, 384), vmem(2, 128, 384),
            vmem(2, 2, 512, 128, dtype=F32), vmem(2, 2, 512, 128), vmem(2, 2, 512, 128),
            vmem(16, 64, 128), vmem(3, 4, 64, 128), vmem(4, 2, 64, 128), vmem(4, 2, 64, 128),
            vmem(2, R, 128), vmem(2, R, 128), vmem(2, 128, R), vmem(128, R), vmem(2, 128, R),
            vmem(2, R, 128, dtype=F32), vmem(2, R, 128, dtype=F32),
            vmem(2, R, BLK, dtype=F32), vmem(2, R, BLK),
            vmem(GRADS, 128), vmem(GRADS, 128), vmem(GRADS // 2, 128),
            vmem(GRADS * 3 // 8, 128), vmem(GRADS // 8, 128), vmem(GRADS * 3 // 32, 128), vmem(GRADS // 8, 128),
            vmem(512, D, dtype=F32),
            dma((4,)), dma((5,)), dma((4,)), dma((4,)), dma((16,)), dma((16,)),
            dma((3, REDUCE_SEMS)), dma((3, REDUCE_SEMS)),
        ],
        compiler_params=pltpu.CompilerParams(vmem_limit_bytes=VMEM, collective_id=0, has_side_effects=True),
        name="layer",
    )(kept, gain, tokens[0], grad_out[0], w, w_out)
    layer, grad_tokens, g_qkv, g_proj, g_gain = pl.pallas_call(
        deliver,
        out_shape=[shape(R, D), shape(R, D), shape(D, 3 * D, dtype=F32), shape(D, D, dtype=F32), shape(D, dtype=F32)],
        in_specs=[A, A, A, V, A],
        out_specs=[A, A, A, A, V],
        scratch_shapes=[
            vmem(2, R, D), vmem(GRADS, 128), vmem(D, 3 * D), vmem(2, R, D), vmem(D, 3 * D, dtype=F32), vmem(D, D, dtype=F32),
            dma((7,)), dma((14,)),
        ],
        compiler_params=pltpu.CompilerParams(vmem_limit_bytes=VMEM),
        name="deliver",
    )(layer_p, tokens_p, gw, gain, w)
    return layer[None], grad_tokens[None], g_qkv, g_proj, g_gain


def solution(mesh):
    in_specs = (P("dp", "ctx", None), P("dp"), P(), P(), P(), P("dp", "ctx", None))
    out_specs = (P("dp", "ctx", None), P("dp", "ctx", None), P(), P(), P())
    return jax.shard_map(shards, mesh=mesh, in_specs=in_specs, out_specs=out_specs, check_vma=False)
```

```python
import functools

import jax
import jax.numpy as jnp
import numpy as np
from jax import lax
from jax.experimental import pallas as pl
from jax.experimental.pallas import tpu as pltpu
from jax.sharding import PartitionSpec as P

BF = jnp.bfloat16
F32 = jnp.float32
LOG2E = 1.4426950408889634
Q_SCALE = 0.125 * LOG2E
NEG = -1e9
R = 1024
D = 768
BLK = 512
FEW = 256
VMEM = 60 * 1024 * 1024


def nn(a, b):
    return lax.dot_general(a, b, (((1,), (0,)), ((), ())), preferred_element_type=F32)


def nt(a, b):
    return lax.dot_general(a, b, (((1,), (1,)), ((), ())), preferred_element_type=F32)


def iota(shape, dim):
    return lax.broadcasted_iota(jnp.int32, shape, dim)


def residue(i):
    return jnp.where(i < 8, 2 * i, 2 * i - 15)


def place(p):
    return 16 * (p & 63) + residue(p >> 6)


def row_order():
    r, c = iota((256, 256), 0), iota((256, 256), 1)
    return jnp.where(c == 16 * (r & 15) + residue(r >> 4), 1.0, 0.0).astype(BF)


def row_order_back():
    c, r = iota((256, 256), 0), iota((256, 256), 1)
    return jnp.where(c == 16 * (r & 15) + residue(r >> 4), 1.0, 0.0).astype(BF)


def head_order():
    r, c = iota((256, 256), 0), iota((256, 256), 1)
    b = c >> 6
    b = jnp.where(b == 1, 2, jnp.where(b == 2, 1, b))
    return jnp.where(r == 64 * b + (c & 63), 1.0, 0.0).astype(BF)


HEAD_BLOCKS = (0, 2, 1, 3)


def diag_mask(x):
    r, c = iota((128, 128), 0), iota((128, 128), 1)
    return jnp.where((r < 64) == (c < 64), x, 0.0)


MESH = pl.DeviceIdType.MESH


def flip(x):
    return jnp.transpose(x.astype(F32)).astype(BF)


def half_turn(x):
    return pltpu.roll(x, 64, 1)


class Links:
    def __init__(self):
        self.dp, self.ctx = lax.axis_index("dp"), lax.axis_index("ctx")
        self.core = self.dp & 1
        self.y, self.x, self.z = self.dp >> 1, self.ctx >> 2, self.ctx & 3

        def low(i):
            return (i ^ (i >> 1)) & 1

        self.groups = (
            (((0, 4), (6, 0)), 2 * low(self.x) + (self.y >> 1)),
            (((2, 0), (0, 3)), 2 * low(self.y) + (self.z >> 1)),
            (((0, 1), (0, 12)), 2 * low(self.z) + (self.x >> 1)),
        )

    def peer(self, group, k):
        (a, b), _ = self.groups[group]
        dp = (a[0] if k & 2 else 0) ^ (b[0] if k & 1 else 0)
        ctx = (a[1] if k & 2 else 0) ^ (b[1] if k & 1 else 0)
        return dp, ctx

    def at(self, flips):
        return (self.dp ^ flips[0], self.ctx ^ flips[1])

    def all_flips(self):
        found = {(1, 0)}
        for k in (1, 2, 3):
            found |= {(0, k), (0, 4 * k)}
            for group in range(3):
                found.add(self.peer(group, k))
        return sorted(found)


def at_rows(start, size):
    return pl.ds(pl.multiple_of(start, 16), size)


class Reduce:
    def __init__(self, links, c, start, size, gw, red, rc, r1, a1, r2, r3, send, recv):
        self.links, self.start, self.gw, self.red = links, start, gw, red
        self.parts = 3
        self.half = size // 2
        self.part = self.half // self.parts
        self.quart, self.small = self.part // 4, self.part // 16
        self.rc = rc.at[pl.ds(start // 2, size // 2)]
        self.r1 = r1.at[pl.ds(start * 3 // 8, size * 3 // 8)]
        self.a1 = a1.at[pl.ds(start // 8, size // 8)]
        self.r2 = r2.at[pl.ds(start * 3 // 32, size * 3 // 32)]
        self.r3 = r3.at[pl.ds(start // 8, size // 8)]
        self.send, self.recv = send.at[c], recv.at[c]
        self.sent = []
        self.waiting = []
        self.mine = start + links.core * self.half
        self.todo = [self.swap, self.scatter1, self.scatter2, self.share, self.gather2, self.gather1, self.swap_back]

    def step(self):
        if self.todo:
            self.todo.pop(0)()

    def copy(self, src, dst, sem, flips):
        copy = pltpu.make_async_remote_copy(
            src_ref=src, dst_ref=dst, send_sem=self.send.at[sem], recv_sem=self.recv.at[sem],
            device_id=self.links.at(flips), device_id_type=MESH,
        )
        copy.start()
        self.sent.append(copy)
        self.waiting.append(copy)

    def arrive(self):
        for copy in self.waiting:
            copy.wait_recv()
        self.waiting = []

    def group(self, stage, part):
        g = (part + stage) % 3
        return g, self.links.groups[g][1]

    def swap(self):
        other = at_rows(self.start + (1 - self.links.core) * self.half, self.half)
        self.copy(self.gw.at[other], self.rc, 0, (1, 0))

    def scatter1(self):
        self.arrive()

        def add(i, _):
            to = at_rows(self.mine + i * 512, 512)
            fr = at_rows(i * 512, 512)
            self.gw[to] = (self.gw[to].astype(F32) + self.rc[fr].astype(F32)).astype(BF)
            return 0

        lax.fori_loop(0, self.half // 512, add, 0)
        for part in range(self.parts):
            g, i = self.group(0, part)
            for k in (1, 2, 3):
                src = self.gw.at[at_rows(self.mine + part * self.part + (i ^ k) * self.quart, self.quart)]
                at = 3 * part + k - 1
                self.copy(src, self.r1.at[pl.ds(at * self.quart, self.quart)], 1 + at, self.links.peer(g, k))

    def scatter2(self):
        self.arrive()
        for part in range(self.parts):
            _, i = self.group(0, part)
            total = self.gw[at_rows(self.mine + part * self.part + i * self.quart, self.quart)].astype(F32)
            for k in range(3):
                at = (3 * part + k) * self.quart
                total += self.r1[at : at + self.quart].astype(F32)
            self.a1[part * self.quart : (part + 1) * self.quart] = total.astype(BF)
            g, i = self.group(1, part)
            for k in (1, 2, 3):
                src = self.a1.at[at_rows(part * self.quart + (i ^ k) * self.small, self.small)]
                at = 3 * part + k - 1
                self.copy(src, self.r2.at[pl.ds(at * self.small, self.small)], 10 + at, self.links.peer(g, k))

    def share(self):
        self.arrive()
        for part in range(self.parts):
            _, i = self.group(1, part)
            total = self.a1[at_rows(part * self.quart + i * self.small, self.small)].astype(F32)
            for k in range(3):
                at = (3 * part + k) * self.small
                total += self.r2[at : at + self.small].astype(F32)
            g, i = self.group(2, part)
            here = at_rows((4 * part + i) * self.small, self.small)
            self.r3[here] = total.astype(BF)
            for k in (1, 2, 3):
                self.copy(self.r3.at[here], self.r3.at[here], 19 + 3 * part + k - 1, self.links.peer(g, k))

    def gather2(self):
        self.arrive()
        for part in range(self.parts):
            total = None
            for k in range(4):
                at = (4 * part + k) * self.small
                x = self.r3[at : at + self.small].astype(F32)
                total = x if total is None else total + x
            g, i2 = self.group(1, part)
            at = at_rows(self.mine + part * self.part + self.group(0, part)[1] * self.quart + i2 * self.small, self.small)
            self.red[at] = total.astype(BF)
            for k in (1, 2, 3):
                self.copy(self.red.at[at], self.red.at[at], 28 + 3 * part + k - 1, self.links.peer(g, k))

    def gather1(self):
        self.arrive()
        for part in range(self.parts):
            g, i = self.group(0, part)
            at = at_rows(self.mine + part * self.part + i * self.quart, self.quart)
            for k in (1, 2, 3):
                self.copy(self.red.at[at], self.red.at[at], 37 + 3 * part + k - 1, self.links.peer(g, k))

    def swap_back(self):
        self.arrive()
        at = at_rows(self.mine, self.half)
        self.copy(self.red.at[at], self.red.at[at], 46, (1, 0))

    def done(self):
        while self.todo:
            self.step()
        self.arrive()


REDUCE_SEMS = 47
UNIT, UNITS = 3072, ((4, 5), (0, 1), (2, 3))
GRADS = 18432


def prepare_keys(slot, kh, vh, k, v, bias, ka, va, vat):
    lane = iota((R, 128), 1)
    ka[slot] = jnp.where((lane < 64) == (kh == 0), k, jnp.where(lane == 64 - 64 * kh, bias, 0.0)).astype(BF)
    other = 64 - 64 * vh
    va_h = jnp.where((lane < 64) == (vh == 0), v, jnp.where((lane == other) | (lane == other + 1), 1.0, 0.0))
    va[slot] = va_h.astype(BF)
    vat[slot] = jnp.transpose(va_h).astype(BF)


def prepare_queries(slot, kh, qt, qa):
    sub = iota(qt.shape, 0)
    x = jnp.where((sub < 64) == (kh == 0), qt.astype(F32), jnp.where(sub == 64 - 64 * kh, 1.0, 0.0))
    qa[slot, :, : qt.shape[1]] = x.astype(BF)


class Attend:
    def __init__(self, slot, kh, vh, add, q, ok, dot_, scr):
        self.slot, self.kh, self.vh, self.add = slot, kh, vh, add
        self.q, self.ok, self.dot_ = q, ok, dot_
        self.width = q.shape[1]
        self.ka, self.va, self.vat, self.kt, _, self.dk, self.dv, self.s_ref, self.p_ref = scr
        self.top = self.o = self.dq = None

    def scores(self, keys):
        s = nn(self.ka[self.slot, keys], self.q)
        self.s_ref[self.slot, keys, : self.width] = s
        m = jnp.max(s, 0, keepdims=True)
        self.top = m if self.top is None else jnp.maximum(self.top, m)

    def mix(self, keys):
        p = jnp.exp2(self.s_ref[self.slot, keys, : self.width] - self.top).astype(BF)
        self.p_ref[self.slot, keys, : self.width] = p
        part = nn(self.vat[self.slot, :, keys], p)
        self.o = part if self.o is None else self.o + part

    def turn(self):
        other, vh = 64 - 64 * self.vh, self.vh
        scale = 1.0 / self.o[other : other + 1]
        self.out = jnp.where(self.ok, self.o[64 * vh : 64 * vh + 64] * scale, 0.0).astype(BF)
        do = self.dot_.astype(F32)
        inner = jnp.sum(do * self.out.astype(F32), 0, keepdims=True) * scale
        high = inner.astype(BF).astype(F32)
        sub = iota((64, self.width), 0)
        extra = jnp.where(sub == 0, -high, jnp.where(sub == 1, high - inner, 0.0))
        parts = [do * scale, extra] if vh == 0 else [extra, do * scale]
        self.da = jnp.concatenate(parts, 0).astype(BF)

    def back(self, keys):
        slot, kh = self.slot, self.kh
        dp = nn(self.va[slot, keys], self.da)
        p = self.p_ref[slot, keys, : self.width]
        ds = (p.astype(F32) * dp).astype(BF)
        if self.add:
            self.dv[slot, keys] += nt(p, self.da)
            self.dk[slot, keys] += nt(ds, self.q)
        else:
            self.dv[slot, keys] = nt(p, self.da)
            self.dk[slot, keys] = nt(ds, self.q)
        part = nn(self.kt[64 * kh : 64 * kh + 64, keys], ds)
        self.dq = part if self.dq is None else self.dq + part

    def results(self):
        return self.out, (self.dq * 0.125).astype(BF)


KEYS = [slice(256 * c, 256 * c + 256) for c in range(4)]


def attend_one(a):
    for keys in KEYS:
        a.scores(keys)
    for keys in KEYS:
        a.mix(keys)
    a.turn()
    for keys in KEYS:
        a.back(keys)


def attend_two(a, b):
    for keys in KEYS:
        a.scores(keys)
    for keys in KEYS:
        a.mix(keys)
        b.scores(keys)
    a.turn()
    for keys in KEYS:
        a.back(keys)
        b.mix(keys)
    b.turn()
    for keys in KEYS:
        b.back(keys)


def join(acc, scale):
    lane = iota((acc.shape[1], 128), 1)
    return jnp.where(lane < 64, acc[0], acc[1]) * scale


def attend_pair(qt, dot_, k, v, bias, limit, start, width, outs, dqs, scr, between=None):
    ka, va, vat, kt, qa, dk, dv, s_ref, p_ref = scr
    k, v = k.astype(F32), v.astype(F32)
    for h in range(2):
        prepare_keys(h, h, h, k, v, bias, ka, va, vat)
        prepare_queries(h, h, qt[...], qa)
    kt[...] = jnp.transpose(k).astype(BF)
    dk[...] = jnp.zeros_like(dk)
    dv[...] = jnp.zeros_like(dv)

    def step(i, _):
        cols = pl.ds(pl.multiple_of(i * BLK, BLK), BLK)
        ok = place(iota((1, BLK), 1) + start + i * BLK) < limit
        two = [Attend(h, h, h, True, qa[h, :, cols], ok, dot_[64 * h : 64 * h + 64, cols], scr) for h in range(2)]
        attend_two(*two)
        for h in range(2):
            outs[64 * h : 64 * h + 64, cols], dqs[64 * h : 64 * h + 64, cols] = two[h].results()
        return 0

    if between is None:
        lax.fori_loop(0, width // BLK, step, 0)
    else:
        i = 0
        for count, action in between:
            lax.fori_loop(i, i + count, step, 0)
            i += count
            if action is not None:
                action()


def blocks_of(first, second):
    first, second = first.astype(F32), second.astype(F32)
    a = diag_mask(jnp.concatenate([first, half_turn(second)], 0))
    b = diag_mask(jnp.concatenate([half_turn(first), second], 0))
    return a, b


def pack_heads(a, b):
    left = iota((64, 128), 1) < 64
    return (
        jnp.where(left, a[:64], half_turn(b[:64])),
        jnp.where(left, half_turn(a[64:]), b[64:]),
    )


def layer_kernel(
    kept, gain_ref, tokens_hbm, grad_hbm, w_hbm, w_out_hbm,
    layer_hbm, gt_hbm, red_hbm,
    tokens, grad_out, w, xp, gp, nm, nmt, wp, wo,
    q0t, k0, v0, do0, q1t, kv1, far1, do1, src2, kv2, qd2,
    o0, o1, dq0, dq1, g1, g2, near, back, back_r, xb2, xr2, zb2, zr2,
    ka, va, vat, kt, qa, dk, dv, ka_b, va_b, vat_b, kt_b, qa_b, dk_b, dv_b, s_ref, p_ref,
    gw, red, rc, r1, a1, r2, r3, u_ref,
    load_sem, store_sem, send1, recv1, send2, recv2, red_send, red_recv,
):
    links = Links()
    me, mx, mz = links.ctx, links.x, links.z
    limit = kept[0] - me * R
    far_limit = kept[0] - (me ^ 1) * R
    gain = gain_ref[...].reshape(1, D)
    barrier = pltpu.get_barrier_semaphore()
    flips = links.all_flips()
    for f in flips:
        pl.semaphore_signal(barrier, inc=1, device_id=links.at(f), device_id_type=MESH)
    loads = []

    def load(src, dst):
        loads.append(pltpu.make_async_copy(src, dst, load_sem.at[len(loads)]))
        loads[-1].start()
        return [loads[-1]]

    def load_columns(level, kind):
        return load(w_hbm.at[:, pl.ds(kind * D + 256 * level, 256)], w.at[3 * level + kind - 3])

    def arrived(copies):
        for copy in copies:
            copy.wait()

    load_x = load(tokens_hbm, tokens)
    load_w1 = load_columns(1, 1) + load_columns(1, 2)
    load_g = load(grad_hbm, grad_out)
    load_w2 = load_columns(1, 0) + load_columns(2, 0) + load_columns(2, 1) + load_columns(2, 2)
    load_wo = load(w_out_hbm.at[pl.ds(0, 256)], wo.at[pl.ds(0, 256)])
    for level in (1, 2):
        for at, block in enumerate(HEAD_BLOCKS):
            load_wo += load(w_out_hbm.at[pl.ds(256 * level + 64 * block, 64)], wo.at[pl.ds(256 * level + 64 * at, 64)])
    load_w0 = []
    for kind in range(3):
        for pair in range(2):
            load_w0 += load(w_hbm.at[:, pl.ds(D * kind + 128 * pair, 128)], wp.at[:, pl.ds(384 * pair + 128 * kind, 128)])
    sent = []

    def push(src, dst, send, recv, flips):
        copy = pltpu.make_async_remote_copy(
            src_ref=src, dst_ref=dst, send_sem=send, recv_sem=recv, device_id=links.at(flips), device_id_type=MESH
        )
        copy.start()
        sent.append(copy)
        return copy

    order = row_order()
    arrived(load_x)
    for t in range(4):
        x = nn(order, tokens[256 * t : 256 * t + 256])
        mean = jnp.mean(x, -1, keepdims=True)
        cent = x - mean
        inv = lax.rsqrt(jnp.mean(cent * cent, -1, keepdims=True) + 1e-05)
        n = (cent * inv * gain).astype(BF)
        xb = x.astype(BF)
        for i in range(16):
            to = slice(64 * i + 16 * t, 64 * i + 16 * t + 16)
            xp[to] = xb[16 * i : 16 * i + 16]
            nm[to] = n[16 * i : 16 * i + 16]
    heads = head_order()
    halves = [slice(0, 512), slice(512, 1024)]
    fews = [slice(0, 128), slice(512, 640)]

    def order_columns(level, kind):
        x = nn(w[3 * level + kind - 3], heads).astype(BF)
        for half in range(2):
            to = 768 * level + 384 * half + 128 * kind
            wp[:, to : to + 128] = x[:, 128 * half : 128 * half + 128]

    arrived(load_w1)
    for kind in (1, 2):
        order_columns(1, kind)
    for half in range(2):
        at = 768 + 384 * half
        x = nn(nm[halves[half]], wp[:, at + 128 : at + 384]).astype(BF)
        kv1[half, 0] = x[:, :128]
        kv1[half, 1] = x[:, 128:]
    pl.semaphore_wait(barrier, len(flips))
    got1 = [push(kv1.at[0], far1.at[0], send1.at[0], recv1.at[0], (0, 1))]

    arrived(load_w2)
    order_columns(1, 0)
    for kind in range(3):
        order_columns(2, kind)
    arrived(load_g)
    for t in range(4):
        gb = nn(order, grad_out[256 * t : 256 * t + 256]).astype(BF)
        for i in range(16):
            gp[64 * i + 16 * t : 64 * i + 16 * t + 16] = gb[16 * i : 16 * i + 16]
    arrived(load_wo)
    for half in range(2):
        at = 1536 + 384 * half
        x = nn(nm[fews[half]], wp[:, at : at + 384])
        do = nt(gp[fews[half]], wo[512 + 128 * half : 640 + 128 * half])
        do = jnp.where(place(iota((128, 128), 0) + 512 * half) < limit, do, 0.0)
        for kind, (a, b) in enumerate(((x[:, 128:256], x[:, 256:]), (x[:, :128] * Q_SCALE, do))):
            first, second = pack_heads(a, b)
            src2[half, kind] = first.astype(BF)
            src2[half + 2, kind] = second.astype(BF)
    kv2[me] = src2[mz, 0]
    qd2[mz] = src2[mz, 1]
    got2 = []
    for k in (1, 2, 3):
        got2.append(push(src2.at[mz ^ k, 0], kv2.at[me], send2.at[k], recv2.at[k], (0, k)))
        got2.append(push(src2.at[mz ^ k, 1], qd2.at[mz], send2.at[3 + k], recv2.at[3 + k], (0, k)))
    got1.append(push(kv1.at[1], far1.at[1], send1.at[1], recv1.at[1], (0, 1)))
    arrived(load_w0)
    for pair in range(2):
        c = slice(128 * pair, 128 * pair + 128)
        x = nn(nm[...], wp[:, 384 * pair : 384 * pair + 384])
        q0t[c] = jnp.transpose(x[:, :128] * Q_SCALE).astype(BF)
        k0[:, c] = x[:, 128:256].astype(BF)
        v0[:, c] = x[:, 256:].astype(BF)
    ok = place(iota((1, R), 1)) < limit
    do0[...] = jnp.where(ok, nt(wo[:256], gp[...]), 0.0).astype(BF)
    nmt[...] = jnp.transpose(nm[...])
    for half in range(2):
        at = 768 + 384 * half
        q1t[half] = jnp.transpose(nn(nm[halves[half]], wp[:, at : at + 128]) * Q_SCALE).astype(BF)
        ok = place(iota((1, 512), 1) + 512 * half) < limit
        do1[half] = jnp.where(ok, nt(wo[256 + 128 * half : 384 + 128 * half], gp[halves[half]]), 0.0).astype(BF)
    plane = pl.ds(4 * mx, 4)
    got_x = []

    def level2_keys():
        for copy in got2:
            copy.wait_recv()
        for k in (1, 2, 3):
            got_x.append(push(kv2.at[plane], kv2.at[plane], send2.at[6 + k], recv2.at[6 + k], (0, 4 * k)))

    reduces = [
        Reduce(links, c, UNIT * c, UNIT, gw, red, rc, r1, a1, r2, r3, red_send, red_recv)
        for c in range(6)
    ]
    active = []

    def tick(count):
        for _ in range(min(count, len(active))):
            r = active.pop(0)
            r.step()
            if r.todo:
                active.append(r)

    def begin(c, x, y):
        for kind in range(3):
            to = UNIT * c + 768 * kind
            gw[to : to + 768] = x[:, 128 * kind : 128 * kind + 128].astype(BF)
        for t in range(6):
            to = UNIT * c + 2304 + 128 * t
            gw[to : to + 128] = y[:, 128 * t : 128 * t + 128].astype(BF)
        reduces[c].step()
        active.append(reduces[c])

    g0 = nm
    scr = (ka, va, vat, kt, qa, dk, dv, s_ref, p_ref)
    scr_b = (ka_b, va_b, vat_b, kt_b, qa_b, dk_b, dv_b, s_ref, p_ref)
    sub = iota((R, 128), 0)
    lane = iota((R, 128), 1)
    bias0 = jnp.where(place(sub) < limit, 0.0, NEG)

    def level0(pair, between):
        c = slice(128 * pair, 128 * pair + 128)
        attend_pair(q0t.at[c], do0.at[c], k0[:, c], v0[:, c], bias0, limit, 0, R, o0.at[c], dq0.at[c], scr, between)
        at = 384 * pair
        g0[:, at : at + 128] = flip(dq0[c])
        g0[:, at + 128 : at + 256] = join(dk, 1.0 / LOG2E).astype(BF)
        g0[:, at + 256 : at + 384] = join(dv, 1.0).astype(BF)
        begin(UNITS[0][pair], nn(nmt[...], g0[:, at : at + 384]), nn(o0[c], gp[...]))

    def level2():
        for copy in got_x:
            copy.wait_recv()
        bias = jnp.where(R * (sub >> 6) + 16 * (sub & 63) + mz < kept[0], 0.0, NEG)
        kv = kv2[...].reshape(R, 128).astype(F32)
        prepare_keys(0, 0, 1, kv, kv, bias, ka_b, va_b, vat_b)
        kt_b[...] = jnp.transpose(kv).astype(BF)
        qdt = flip(qd2[...].reshape(256, 128))
        prepare_queries(0, 0, qdt, qa_b)
        col = iota((1, FEW), 1)
        ok = R * (4 * mx + (col >> 6)) + 16 * (col & 63) + mz < kept[0]
        head = Attend(0, 0, 1, False, qa_b[0, :, :FEW], ok, qdt[64:], scr_b)
        attend_one(head)
        o, dq = head.results()
        zb2[:, 1] = flip(jnp.concatenate([o, dq], 0)).reshape(4, 64, 128)
        xb2[...] = jnp.where(lane < 64, dk_b[0] * (1.0 / LOG2E), dv_b[0]).astype(BF).reshape(16, 64, 128)
        got_x[:] = [
            push(xb2.at[pl.ds(4 * (mx ^ k), 4)], xr2.at[k - 1], send2.at[9 + k], recv2.at[9 + k], (0, 4 * k)) for k in (1, 2, 3)
        ]

    got_z = []

    def level2_back():
        for copy in got_x:
            copy.wait_recv()
        total = xb2[plane].astype(F32)
        for k in range(3):
            total += xr2[k].astype(F32)
        zb2[:, 0] = total.astype(BF)
        zr2[mz] = zb2[mz]
        for k in (1, 2, 3):
            got_z.append(push(zb2.at[mz ^ k], zr2.at[mz], send2.at[12 + k], recv2.at[12 + k], (0, k)))

    outs2 = []

    def level2_grads():
        for copy in got_z:
            copy.wait_recv()
        for half in range(2):
            o, dq = blocks_of(zr2[half, 1], zr2[half + 2, 1])
            outs2.append(o.astype(BF))
            gk, gv = blocks_of(zr2[half, 0], zr2[half + 2, 0])
            for kind, x in enumerate((dq, gk, gv)):
                g2[half, :, 128 * kind : 128 * kind + 128] = x.astype(BF)
            begin(UNITS[2][half], nn(nmt[:, fews[half]], g2[half]), nn(jnp.transpose(o).astype(BF), gp[fews[half]]))

    got_back1 = []

    def level1(half):
        rows = halves[half]
        at = place((sub & 511) + 512 * half)
        bias = jnp.where(at < jnp.where(sub < 512, limit, far_limit), 0.0, NEG)
        got1[half].wait_recv()
        k = jnp.concatenate([kv1[half, 0], far1[half, 0]], 0)
        v = jnp.concatenate([kv1[half, 1], far1[half, 1]], 0)
        attend_pair(q1t.at[half], do1.at[half], k, v, bias, limit, 512 * half, 512, o1.at[half], dq1.at[half], scr_b)
        gk = join(dk_b, 1.0 / LOG2E)
        gv = join(dv_b, 1.0)
        near[half, 0] = gk[:512]
        near[half, 1] = gv[:512]
        back[half, 0] = gk[512:].astype(BF)
        back[half, 1] = gv[512:].astype(BF)
        if half == 1:
            level2_back()
        got_back1.append(push(back.at[half], back_r.at[half], send1.at[2 + half], recv1.at[2 + half], (0, 1)))

    def level1_grads(half):
        got_back1[half].wait_recv()
        g1[halves[half], :128] = flip(dq1[half])
        for kind in range(2):
            total = near[half, kind] + back_r[half, kind].astype(F32)
            g1[halves[half], 128 + 128 * kind : 256 + 128 * kind] = total.astype(BF)
        begin(UNITS[1][half], nn(nmt[:, halves[half]], g1[halves[half]]), nn(o1[half], gp[halves[half]]))

    def middle():
        level2_keys()
        level1(0)
        level2()
        level1(1)

    def gap():
        tick(4)
        level1_grads(1)

    level0(0, [(1, middle), (1, None)])
    level2_grads()
    level1_grads(0)
    level0(1, [(1, gap), (1, lambda: tick(5))])

    for half in range(2):
        rows = halves[half]
        at = 768 + 384 * half
        u_ref[...] = nt(g0[rows], wp[:, :768])
        u_ref[...] += nt(g1[rows], wp[:, at : at + 384])
        u_ref[:128] += nt(g2[half], wp[:, 768 + at : 1152 + at])
        tick(2)
        for t in range(4):
            here = slice(512 * half + 128 * t, 512 * half + 128 * t + 128)
            x = xp[here].astype(F32)
            u = u_ref[128 * t : 128 * t + 128] * gain
            cent = x - jnp.mean(x, -1, keepdims=True)
            inv = lax.rsqrt(jnp.mean(cent * cent, -1, keepdims=True) + 1e-05)
            xhat = cent * inv
            mean = jnp.mean(u, -1, keepdims=True)
            dotted = jnp.mean(u * xhat, -1, keepdims=True)
            grad_out[here] = (gp[here].astype(F32) + inv * (u - mean - xhat * dotted)).astype(BF)
        tick(2)
        u_ref[...] = nn(flip(o0[:, rows]), wo[:256]) + nn(flip(o1[half]), wo[256 + 128 * half : 384 + 128 * half])
        u_ref[:128] += nn(outs2[half], wo[512 + 128 * half : 640 + 128 * half])
        tokens[rows] = (xp[rows].astype(F32) + u_ref[...]).astype(BF)
        tick(2)
    stores = [
        pltpu.make_async_copy(tokens, layer_hbm, store_sem.at[0]),
        pltpu.make_async_copy(grad_out, gt_hbm, store_sem.at[1]),
    ]
    for store in stores:
        store.start()
    while active:
        tick(1)
    for c in (4, 0, 1, 2, 3, 5):
        reduces[c].done()
        rows = slice(UNIT * c, UNIT * c + UNIT)
        stores.append(pltpu.make_async_copy(red.at[rows], red_hbm.at[rows], store_sem.at[2 + c]))
        stores[-1].start()
        sent.extend(reduces[c].sent)
    for copy in sent:
        copy.wait_send()
    for store in stores:
        store.wait()


def deliver(
    layer_in, tokens_in, gw_in, gain, w_in, layer_out, tokens_out, qkv_out, proj_out, g_gain,
    src, gw, w, dst, qkv, proj, load_sem, store_sem,
):
    loads = [pltpu.make_async_copy(x, src.at[i], load_sem.at[i]) for i, x in enumerate((layer_in, tokens_in))]
    for level in range(3):
        rows = pl.ds(UNIT * UNITS[level][0], 2 * UNIT)
        loads.append(pltpu.make_async_copy(gw_in.at[rows], gw.at[rows], load_sem.at[2 + level]))
    loads.append(pltpu.make_async_copy(w_in, w, load_sem.at[5]))
    for load in loads:
        load.start()
    stores = []

    def store(x, y):
        stores.append(pltpu.make_async_copy(x, y, store_sem.at[len(stores)]))
        stores[-1].start()

    order = row_order_back()
    for i, out in enumerate((layer_out, tokens_out)):
        loads[i].wait()
        for t in range(4):
            x = jnp.concatenate([src[i, 64 * j + 16 * t : 64 * j + 16 * t + 16] for j in range(16)], 0)
            dst[i, 256 * t : 256 * t + 256] = nn(order, x).astype(BF)
        store(dst.at[i], out)
    heads = head_order()
    total = jnp.zeros((D, 128), F32)
    loads[5].wait()
    for level in range(3):
        loads[2 + level].wait()
        for kind in range(3):
            ats = [UNIT * unit + 768 * kind for unit in UNITS[level]]
            x = jnp.concatenate([gw[at : at + 768] for at in ats], 1)
            x = x.astype(F32) if level == 0 else nn(x, heads)
            c = slice(D * kind + 256 * level, D * kind + 256 * level + 256)
            qkv[:, c] = x
            store(qkv.at[:, c], qkv_out.at[:, c])
            prod = x * w[:, c].astype(F32)
            total += prod[:, :128] + prod[:, 128:]
        for t in range(6):
            for i, block in enumerate((0, 1, 2, 3) if level == 0 else HEAD_BLOCKS):
                at = UNIT * UNITS[level][i // 2] + 2304 + 128 * t + 64 * (i % 2)
                to = 256 * level + 64 * block
                proj[to : to + 64, 128 * t : 128 * t + 128] = gw[at : at + 64].astype(F32)
        rows = pl.ds(256 * level, 256)
        store(proj.at[rows], proj_out.at[rows])
    g_gain[...] = (jnp.sum(jnp.transpose(total), 0, keepdims=True) / gain[...].reshape(1, D)).reshape(D)
    for copy in stores:
        copy.wait()


def shape(*dims, dtype=BF):
    return jax.ShapeDtypeStruct(dims, dtype)


V = pl.BlockSpec(memory_space=pltpu.VMEM)
S = pl.BlockSpec(memory_space=pltpu.SMEM)
A = pl.BlockSpec(memory_space=pl.ANY)


def vmem(*dims, dtype=BF):
    return pltpu.VMEM(dims, dtype)


def shards(tokens, kept, gain, w, w_out, grad_out):
    dma = pltpu.SemaphoreType.DMA
    layer_p, tokens_p, gw = pl.pallas_call(
        layer_kernel,
        out_shape=[shape(R, D), shape(R, D), shape(GRADS, 128)],
        in_specs=[S, V] + [A] * 4,
        out_specs=[A] * 3,
        scratch_shapes=[
            vmem(R, D), vmem(R, D), vmem(6, D, 256), vmem(R, D), vmem(R, D), vmem(R, D), vmem(D, R),
            vmem(D, 3 * D), vmem(D, D),
            vmem(256, R), vmem(R, 256), vmem(R, 256), vmem(256, R),
            vmem(2, 128, 512), vmem(2, 2, 512, 128), vmem(2, 2, 512, 128), vmem(2, 128, 512),
            vmem(4, 2, 64, 128), vmem(16, 64, 128), vmem(4, 64, 128),
            vmem(256, R), vmem(2, 128, 512), vmem(256, R), vmem(2, 128, 512),
            vmem(R, 384), vmem(2, 128, 384),
            vmem(2, 2, 512, 128, dtype=F32), vmem(2, 2, 512, 128), vmem(2, 2, 512, 128),
            vmem(16, 64, 128), vmem(3, 4, 64, 128), vmem(4, 2, 64, 128), vmem(4, 2, 64, 128),
            vmem(2, R, 128), vmem(2, R, 128), vmem(2, 128, R), vmem(128, R), vmem(2, 128, R),
            vmem(2, R, 128, dtype=F32), vmem(2, R, 128, dtype=F32),
            vmem(2, R, 128), vmem(2, R, 128), vmem(2, 128, R), vmem(128, R), vmem(2, 128, 512),
            vmem(2, R, 128, dtype=F32), vmem(2, R, 128, dtype=F32),
            vmem(2, R, BLK, dtype=F32), vmem(2, R, BLK),
            vmem(GRADS, 128), vmem(GRADS, 128), vmem(GRADS // 2, 128),
            vmem(GRADS * 3 // 8, 128), vmem(GRADS // 8, 128), vmem(GRADS * 3 // 32, 128), vmem(GRADS // 8, 128),
            vmem(512, D, dtype=F32),
            dma((25,)), dma((8,)), dma((4,)), dma((4,)), dma((16,)), dma((16,)),
            dma((6, REDUCE_SEMS)), dma((6, REDUCE_SEMS)),
        ],
        compiler_params=pltpu.CompilerParams(vmem_limit_bytes=VMEM, collective_id=0, has_side_effects=True),
        name="layer",
    )(kept, gain, tokens[0], grad_out[0], w, w_out)
    layer, grad_tokens, g_qkv, g_proj, g_gain = pl.pallas_call(
        deliver,
        out_shape=[shape(R, D), shape(R, D), shape(D, 3 * D, dtype=F32), shape(D, D, dtype=F32), shape(D, dtype=F32)],
        in_specs=[A, A, A, V, A],
        out_specs=[A, A, A, A, V],
        scratch_shapes=[
            vmem(2, R, D), vmem(GRADS, 128), vmem(D, 3 * D), vmem(2, R, D), vmem(D, 3 * D, dtype=F32), vmem(D, D, dtype=F32),
            dma((6,)), dma((14,)),
        ],
        compiler_params=pltpu.CompilerParams(vmem_limit_bytes=VMEM),
        name="deliver",
    )(layer_p, tokens_p, gw, gain, w)
    return layer[None], grad_tokens[None], g_qkv, g_proj, g_gain


def solution(mesh):
    in_specs = (P("dp", "ctx", None), P("dp"), P(), P(), P(), P("dp", "ctx", None))
    out_specs = (P("dp", "ctx", None), P("dp", "ctx", None), P(), P(), P())
    return jax.shard_map(shards, mesh=mesh, in_specs=in_specs, out_specs=out_specs, check_vma=False)
```

```python
import functools

import jax
import jax.numpy as jnp
import numpy as np
from jax import lax
from jax.experimental import pallas as pl
from jax.experimental.pallas import tpu as pltpu
from jax.sharding import PartitionSpec as P

BF = jnp.bfloat16
F32 = jnp.float32
LOG2E = 1.4426950408889634
Q_SCALE = 0.125 * LOG2E
NEG = -1e9
R = 1024
D = 768
BLK = 512
FEW = 256
VMEM = 60 * 1024 * 1024


def nn(a, b):
    return lax.dot_general(a, b, (((1,), (0,)), ((), ())), preferred_element_type=F32)


def nt(a, b):
    return lax.dot_general(a, b, (((1,), (1,)), ((), ())), preferred_element_type=F32)


def iota(shape, dim):
    return lax.broadcasted_iota(jnp.int32, shape, dim)


def residue(i):
    return jnp.where(i < 8, 2 * i, 2 * i - 15)


def place(p):
    return 16 * (p & 63) + residue(p >> 6)


def row_order():
    r, c = iota((256, 256), 0), iota((256, 256), 1)
    return jnp.where(c == 16 * (r & 15) + residue(r >> 4), 1.0, 0.0).astype(BF)


def row_order_back():
    c, r = iota((256, 256), 0), iota((256, 256), 1)
    return jnp.where(c == 16 * (r & 15) + residue(r >> 4), 1.0, 0.0).astype(BF)


def head_order():
    r, c = iota((256, 256), 0), iota((256, 256), 1)
    b = c >> 6
    b = jnp.where(b == 1, 2, jnp.where(b == 2, 1, b))
    return jnp.where(r == 64 * b + (c & 63), 1.0, 0.0).astype(BF)


HEAD_BLOCKS = (0, 2, 1, 3)


def diag_mask(x):
    r, c = iota((128, 128), 0), iota((128, 128), 1)
    return jnp.where((r < 64) == (c < 64), x, 0.0)


MESH = pl.DeviceIdType.MESH


def flip(x):
    return jnp.transpose(x.astype(F32)).astype(BF)


def half_turn(x):
    return pltpu.roll(x, 64, 1)


class Links:
    def __init__(self):
        self.dp, self.ctx = lax.axis_index("dp"), lax.axis_index("ctx")
        self.core = self.dp & 1
        self.y, self.x, self.z = self.dp >> 1, self.ctx >> 2, self.ctx & 3

        def low(i):
            return (i ^ (i >> 1)) & 1

        self.groups = (
            (((0, 4), (6, 0)), 2 * low(self.x) + (self.y >> 1)),
            (((2, 0), (0, 3)), 2 * low(self.y) + (self.z >> 1)),
            (((0, 1), (0, 12)), 2 * low(self.z) + (self.x >> 1)),
        )

    def peer(self, group, k, core=0):
        (a, b), _ = self.groups[group]
        dp = (a[0] if k & 2 else 0) ^ (b[0] if k & 1 else 0)
        ctx = (a[1] if k & 2 else 0) ^ (b[1] if k & 1 else 0)
        return dp ^ core, ctx

    def at(self, flips):
        return (self.dp ^ flips[0], self.ctx ^ flips[1])

    def all_flips(self):
        found = {(1, 0)}
        for k in (1, 2, 3):
            found |= {(0, k), (0, 4 * k)}
            for group in range(3):
                found.add(self.peer(group, k))
                found.add(self.peer(group, k, 1))
        return sorted(found)


def at_rows(start, size):
    return pl.ds(pl.multiple_of(start, 16), size)


class Reduce:
    def __init__(self, links, c, start, size, gw, red, rc, r1, a1, r2, r3, send, recv):
        self.links, self.start, self.gw, self.red = links, start, gw, red
        self.parts = 3
        self.direct = c == 5
        cores = 1 if self.direct else 2
        self.slots = 8 if self.direct else 4
        self.half = size // cores
        self.part = self.half // self.parts
        self.quart, self.small = self.part // 4, self.part // 16
        self.rc = rc.at[pl.ds(start // 2, size // 2)]
        self.r1 = r1.at[pl.ds(start * 3 // 8, 9 * self.quart)]
        self.a1 = a1.at[pl.ds(start // 8, 3 * self.quart)]
        self.r2 = r2.at[pl.ds(start * 3 // 32, 9 * self.small)]
        self.r3 = r3.at[pl.ds(start // 8, 3 * self.slots * self.small)]
        self.send, self.recv = send.at[c], recv.at[c]
        self.sent = []
        self.waiting = []
        self.mine = start if self.direct else start + links.core * self.half
        self.todo = [self.swap, self.scatter1, self.scatter2, self.share, self.gather2, self.gather1, self.swap_back]
        if self.direct:
            self.todo = [self.scatter1, self.scatter2, self.share, self.gather2, self.gather1]

    def step(self):
        if self.todo:
            self.todo.pop(0)()

    def copy(self, src, dst, sem, flips):
        copy = pltpu.make_async_remote_copy(
            src_ref=src, dst_ref=dst, send_sem=self.send.at[sem], recv_sem=self.recv.at[sem],
            device_id=self.links.at(flips), device_id_type=MESH,
        )
        copy.start()
        self.sent.append(copy)
        self.waiting.append(copy)

    def arrive(self):
        for copy in self.waiting:
            copy.wait_recv()
        self.waiting = []

    def group(self, stage, part):
        g = (part + stage) % 3
        return g, self.links.groups[g][1]

    def swap(self):
        other = at_rows(self.start + (1 - self.links.core) * self.half, self.half)
        self.copy(self.gw.at[other], self.rc, 0, (1, 0))

    def scatter1(self):
        self.arrive()

        def add(i, _):
            to = at_rows(self.mine + i * 512, 512)
            fr = at_rows(i * 512, 512)
            self.gw[to] = (self.gw[to].astype(F32) + self.rc[fr].astype(F32)).astype(BF)
            return 0

        if not self.direct:
            lax.fori_loop(0, self.half // 512, add, 0)
        for part in range(self.parts):
            g, i = self.group(0, part)
            for k in (1, 2, 3):
                src = self.gw.at[at_rows(self.mine + part * self.part + (i ^ k) * self.quart, self.quart)]
                at = 3 * part + k - 1
                self.copy(src, self.r1.at[pl.ds(at * self.quart, self.quart)], 1 + at, self.links.peer(g, k))

    def scatter2(self):
        self.arrive()
        for part in range(self.parts):
            _, i = self.group(0, part)
            total = self.gw[at_rows(self.mine + part * self.part + i * self.quart, self.quart)].astype(F32)
            for k in range(3):
                at = (3 * part + k) * self.quart
                total += self.r1[at : at + self.quart].astype(F32)
            self.a1[part * self.quart : (part + 1) * self.quart] = total.astype(BF)
            g, i = self.group(1, part)
            for k in (1, 2, 3):
                src = self.a1.at[at_rows(part * self.quart + (i ^ k) * self.small, self.small)]
                at = 3 * part + k - 1
                self.copy(src, self.r2.at[pl.ds(at * self.small, self.small)], 10 + at, self.links.peer(g, k))

    def share(self):
        self.arrive()
        for part in range(self.parts):
            _, i = self.group(1, part)
            total = self.a1[at_rows(part * self.quart + i * self.small, self.small)].astype(F32)
            for k in range(3):
                at = (3 * part + k) * self.small
                total += self.r2[at : at + self.small].astype(F32)
            g, i = self.group(2, part)
            if self.direct:
                i = i + 4 * self.links.core
            here = at_rows((self.slots * part + i) * self.small, self.small)
            self.r3[here] = total.astype(BF)
            for k in (1, 2, 3):
                self.copy(self.r3.at[here], self.r3.at[here], 19 + 3 * part + k - 1, self.links.peer(g, k))
            if self.direct:
                for k in range(4):
                    self.copy(self.r3.at[here], self.r3.at[here], 47 + 4 * part + k, self.links.peer(g, k, 1))

    def gather2(self):
        self.arrive()
        for part in range(self.parts):
            total = None
            for k in range(self.slots):
                at = (self.slots * part + k) * self.small
                x = self.r3[at : at + self.small].astype(F32)
                total = x if total is None else total + x
            g, i2 = self.group(1, part)
            at = at_rows(self.mine + part * self.part + self.group(0, part)[1] * self.quart + i2 * self.small, self.small)
            self.red[at] = total.astype(BF)
            for k in (1, 2, 3):
                self.copy(self.red.at[at], self.red.at[at], 28 + 3 * part + k - 1, self.links.peer(g, k))

    def gather1(self):
        self.arrive()
        for part in range(self.parts):
            g, i = self.group(0, part)
            at = at_rows(self.mine + part * self.part + i * self.quart, self.quart)
            for k in (1, 2, 3):
                self.copy(self.red.at[at], self.red.at[at], 37 + 3 * part + k - 1, self.links.peer(g, k))

    def swap_back(self):
        self.arrive()
        at = at_rows(self.mine, self.half)
        self.copy(self.red.at[at], self.red.at[at], 46, (1, 0))

    def done(self):
        while self.todo:
            self.step()
        self.arrive()


REDUCE_SEMS = 59
UNIT, UNITS = 3072, ((4, 5), (0, 1), (2, 3))
GRADS = 18432


def prepare_keys(slot, kh, vh, k, v, bias, ka, va, vat):
    lane = iota((R, 128), 1)
    ka[slot] = jnp.where((lane < 64) == (kh == 0), k, jnp.where(lane == 64 - 64 * kh, bias, 0.0)).astype(BF)
    other = 64 - 64 * vh
    va_h = jnp.where((lane < 64) == (vh == 0), v, jnp.where((lane == other) | (lane == other + 1), 1.0, 0.0))
    va[slot] = va_h.astype(BF)
    vat[slot] = jnp.transpose(va_h).astype(BF)


def prepare_queries(slot, kh, qt, qa):
    sub = iota(qt.shape, 0)
    x = jnp.where((sub < 64) == (kh == 0), qt.astype(F32), jnp.where(sub == 64 - 64 * kh, 1.0, 0.0))
    qa[slot, :, : qt.shape[1]] = x.astype(BF)


class Attend:
    def __init__(self, slot, kh, vh, add, q, ok, dot_, scr):
        self.slot, self.kh, self.vh, self.add = slot, kh, vh, add
        self.q, self.ok, self.dot_ = q, ok, dot_
        self.width = q.shape[1]
        self.ka, self.va, self.vat, self.kt, _, self.dk, self.dv, self.s_ref, self.p_ref = scr
        self.top = self.o = self.dq = None

    def scores(self, keys):
        s = nn(self.ka[self.slot, keys], self.q)
        self.s_ref[self.slot, keys, : self.width] = s
        m = jnp.max(s, 0, keepdims=True)
        self.top = m if self.top is None else jnp.maximum(self.top, m)

    def mix(self, keys):
        p = jnp.exp2(self.s_ref[self.slot, keys, : self.width] - self.top).astype(BF)
        self.p_ref[self.slot, keys, : self.width] = p
        part = nn(self.vat[self.slot, :, keys], p)
        self.o = part if self.o is None else self.o + part

    def turn(self):
        other, vh = 64 - 64 * self.vh, self.vh
        scale = 1.0 / self.o[other : other + 1]
        self.out = jnp.where(self.ok, self.o[64 * vh : 64 * vh + 64] * scale, 0.0).astype(BF)
        do = self.dot_.astype(F32)
        inner = jnp.sum(do * self.out.astype(F32), 0, keepdims=True) * scale
        high = inner.astype(BF).astype(F32)
        sub = iota((64, self.width), 0)
        extra = jnp.where(sub == 0, -high, jnp.where(sub == 1, high - inner, 0.0))
        parts = [do * scale, extra] if vh == 0 else [extra, do * scale]
        self.da = jnp.concatenate(parts, 0).astype(BF)

    def back(self, keys):
        slot, kh = self.slot, self.kh
        dp = nn(self.va[slot, keys], self.da)
        p = self.p_ref[slot, keys, : self.width]
        ds = (p.astype(F32) * dp).astype(BF)
        if self.add:
            self.dv[slot, keys] += nt(p, self.da)
            self.dk[slot, keys] += nt(ds, self.q)
        else:
            self.dv[slot, keys] = nt(p, self.da)
            self.dk[slot, keys] = nt(ds, self.q)
        part = nn(self.kt[64 * kh : 64 * kh + 64, keys], ds)
        self.dq = part if self.dq is None else self.dq + part

    def results(self):
        return self.out, (self.dq * 0.125).astype(BF)


KEYS = [slice(256 * c, 256 * c + 256) for c in range(4)]


def attend_one(a):
    for keys in KEYS:
        a.scores(keys)
    for keys in KEYS:
        a.mix(keys)
    a.turn()
    for keys in KEYS:
        a.back(keys)


def attend_two(a, b):
    for keys in KEYS:
        a.scores(keys)
    for keys in KEYS:
        a.mix(keys)
        b.scores(keys)
    a.turn()
    for keys in KEYS:
        a.back(keys)
        b.mix(keys)
    b.turn()
    for keys in KEYS:
        b.back(keys)


def join(acc, scale):
    lane = iota((acc.shape[1], 128), 1)
    return jnp.where(lane < 64, acc[0], acc[1]) * scale


def attend_pair(qt, dot_, k, v, bias, limit, start, width, outs, dqs, scr, between=None):
    ka, va, vat, kt, qa, dk, dv, s_ref, p_ref = scr
    k, v = k.astype(F32), v.astype(F32)
    for h in range(2):
        prepare_keys(h, h, h, k, v, bias, ka, va, vat)
        prepare_queries(h, h, qt[...], qa)
    kt[...] = jnp.transpose(k).astype(BF)
    dk[...] = jnp.zeros_like(dk)
    dv[...] = jnp.zeros_like(dv)

    def step(i, _):
        cols = pl.ds(pl.multiple_of(i * BLK, BLK), BLK)
        ok = place(iota((1, BLK), 1) + start + i * BLK) < limit
        two = [Attend(h, h, h, True, qa[h, :, cols], ok, dot_[64 * h : 64 * h + 64, cols], scr) for h in range(2)]
        attend_two(*two)
        for h in range(2):
            outs[64 * h : 64 * h + 64, cols], dqs[64 * h : 64 * h + 64, cols] = two[h].results()
        return 0

    if between is None:
        lax.fori_loop(0, width // BLK, step, 0)
    else:
        i = 0
        for count, action in between:
            lax.fori_loop(i, i + count, step, 0)
            i += count
            if action is not None:
                action()


def blocks_of(first, second):
    first, second = first.astype(F32), second.astype(F32)
    a = diag_mask(jnp.concatenate([first, half_turn(second)], 0))
    b = diag_mask(jnp.concatenate([half_turn(first), second], 0))
    return a, b


def pack_heads(a, b):
    left = iota((64, 128), 1) < 64
    return (
        jnp.where(left, a[:64], half_turn(b[:64])),
        jnp.where(left, half_turn(a[64:]), b[64:]),
    )


def layer_kernel(
    kept, gain_ref, tokens_hbm, grad_hbm, w_hbm, w_out_hbm,
    layer_hbm, gt_hbm, red_hbm, g_gain,
    tokens, grad_out, w, xp, gp, nm, nmt, wp, wo,
    q0t, k0, v0, do0, q1t, kv1, far1, do1, src2, kv2, qd2,
    o0, o1, dq0, dq1, g1, g2, near, back, back_r, xb2, xr2, zb2, zr2,
    ka, va, vat, kt, qa, dk, dv, ka_b, va_b, vat_b, kt_b, qa_b, dk_b, dv_b, s_ref, p_ref,
    gw, red, rc, r1, a1, r2, r3, u_ref,
    load_sem, store_sem, send1, recv1, send2, recv2, red_send, red_recv,
):
    links = Links()
    me, mx, mz = links.ctx, links.x, links.z
    limit = kept[0] - me * R
    far_limit = kept[0] - (me ^ 1) * R
    gain = gain_ref[...].reshape(1, D)
    barrier = pltpu.get_barrier_semaphore()
    flips = links.all_flips()
    for f in flips:
        pl.semaphore_signal(barrier, inc=1, device_id=links.at(f), device_id_type=MESH)
    loads = []

    def load(src, dst):
        loads.append(pltpu.make_async_copy(src, dst, load_sem.at[len(loads)]))
        loads[-1].start()
        return [loads[-1]]

    def load_columns(level, kind):
        return load(w_hbm.at[:, pl.ds(kind * D + 256 * level, 256)], w.at[3 * level + kind - 3])

    def arrived(copies):
        for copy in copies:
            copy.wait()

    load_x = load(tokens_hbm, tokens)
    load_w1 = load_columns(1, 1) + load_columns(1, 2)
    load_g = load(grad_hbm, grad_out)
    load_w2 = load_columns(1, 0) + load_columns(2, 0) + load_columns(2, 1) + load_columns(2, 2)
    load_wo = load(w_out_hbm.at[pl.ds(0, 256)], wo.at[pl.ds(0, 256)])
    for level in (1, 2):
        for at, block in enumerate(HEAD_BLOCKS):
            load_wo += load(w_out_hbm.at[pl.ds(256 * level + 64 * block, 64)], wo.at[pl.ds(256 * level + 64 * at, 64)])
    load_w0 = []
    for kind in range(3):
        for pair in range(2):
            load_w0 += load(w_hbm.at[:, pl.ds(D * kind + 128 * pair, 128)], wp.at[:, pl.ds(384 * pair + 128 * kind, 128)])
    sent = []

    def push(src, dst, send, recv, flips):
        copy = pltpu.make_async_remote_copy(
            src_ref=src, dst_ref=dst, send_sem=send, recv_sem=recv, device_id=links.at(flips), device_id_type=MESH
        )
        copy.start()
        sent.append(copy)
        return copy

    order = row_order()
    arrived(load_x)
    for t in range(4):
        x = nn(order, tokens[256 * t : 256 * t + 256])
        mean = jnp.mean(x, -1, keepdims=True)
        cent = x - mean
        inv = lax.rsqrt(jnp.mean(cent * cent, -1, keepdims=True) + 1e-05)
        n = (cent * inv * gain).astype(BF)
        xb = x.astype(BF)
        for i in range(16):
            to = slice(64 * i + 16 * t, 64 * i + 16 * t + 16)
            xp[to] = xb[16 * i : 16 * i + 16]
            nm[to] = n[16 * i : 16 * i + 16]
    heads = head_order()
    halves = [slice(0, 512), slice(512, 1024)]
    fews = [slice(0, 128), slice(512, 640)]

    def order_columns(level, kind):
        x = nn(w[3 * level + kind - 3], heads).astype(BF)
        for half in range(2):
            to = 768 * level + 384 * half + 128 * kind
            wp[:, to : to + 128] = x[:, 128 * half : 128 * half + 128]

    arrived(load_w1)
    for kind in (1, 2):
        order_columns(1, kind)
    for half in range(2):
        at = 768 + 384 * half
        x = nn(nm[halves[half]], wp[:, at + 128 : at + 384]).astype(BF)
        kv1[half, 0] = x[:, :128]
        kv1[half, 1] = x[:, 128:]
    pl.semaphore_wait(barrier, len(flips))
    got1 = [push(kv1.at[0], far1.at[0], send1.at[0], recv1.at[0], (0, 1))]

    arrived(load_w2)
    order_columns(1, 0)
    for kind in range(3):
        order_columns(2, kind)
    arrived(load_g)
    for t in range(4):
        gb = nn(order, grad_out[256 * t : 256 * t + 256]).astype(BF)
        for i in range(16):
            gp[64 * i + 16 * t : 64 * i + 16 * t + 16] = gb[16 * i : 16 * i + 16]
    arrived(load_wo)
    for half in range(2):
        at = 1536 + 384 * half
        x = nn(nm[fews[half]], wp[:, at : at + 384])
        do = nt(gp[fews[half]], wo[512 + 128 * half : 640 + 128 * half])
        do = jnp.where(place(iota((128, 128), 0) + 512 * half) < limit, do, 0.0)
        for kind, (a, b) in enumerate(((x[:, 128:256], x[:, 256:]), (x[:, :128] * Q_SCALE, do))):
            first, second = pack_heads(a, b)
            src2[half, kind] = first.astype(BF)
            src2[half + 2, kind] = second.astype(BF)
    kv2[me] = src2[mz, 0]
    qd2[mz] = src2[mz, 1]
    got2 = []
    for k in (1, 2, 3):
        got2.append(push(src2.at[mz ^ k, 0], kv2.at[me], send2.at[k], recv2.at[k], (0, k)))
        got2.append(push(src2.at[mz ^ k, 1], qd2.at[mz], send2.at[3 + k], recv2.at[3 + k], (0, k)))
    got1.append(push(kv1.at[1], far1.at[1], send1.at[1], recv1.at[1], (0, 1)))
    arrived(load_w0)
    for pair in range(2):
        c = slice(128 * pair, 128 * pair + 128)
        x = nn(nm[...], wp[:, 384 * pair : 384 * pair + 384])
        q0t[c] = jnp.transpose(x[:, :128] * Q_SCALE).astype(BF)
        k0[:, c] = x[:, 128:256].astype(BF)
        v0[:, c] = x[:, 256:].astype(BF)
    ok = place(iota((1, R), 1)) < limit
    do0[...] = jnp.where(ok, nt(wo[:256], gp[...]), 0.0).astype(BF)
    nmt[...] = jnp.transpose(nm[...])
    for half in range(2):
        at = 768 + 384 * half
        q1t[half] = jnp.transpose(nn(nm[halves[half]], wp[:, at : at + 128]) * Q_SCALE).astype(BF)
        ok = place(iota((1, 512), 1) + 512 * half) < limit
        do1[half] = jnp.where(ok, nt(wo[256 + 128 * half : 384 + 128 * half], gp[halves[half]]), 0.0).astype(BF)
    plane = pl.ds(4 * mx, 4)
    got_x = []

    def level2_keys():
        for copy in got2:
            copy.wait_recv()
        for k in (1, 2, 3):
            got_x.append(push(kv2.at[plane], kv2.at[plane], send2.at[6 + k], recv2.at[6 + k], (0, 4 * k)))

    reduces = [
        Reduce(links, c, UNIT * c, UNIT, gw, red, rc, r1, a1, r2, r3, red_send, red_recv)
        for c in range(6)
    ]
    active = []
    stores = []

    def store(src, dst):
        stores.append(pltpu.make_async_copy(src, dst, store_sem.at[len(stores)]))
        stores[-1].start()

    def complete(r):
        r.done()
        rows = pl.ds(r.start, UNIT)
        store(red.at[rows], red_hbm.at[rows])
        at = 384 * ((r.start // UNIT + 2) % 6)
        total = dk[0, :D]
        for kind in range(3):
            x = red[r.start + D * kind : r.start + D * kind + D].astype(F32)
            total += x * wp[:, at + 128 * kind : at + 128 * kind + 128].astype(F32)
        dk[0, :D] = total
        sent.extend(r.sent)

    def tick(count):
        for _ in range(min(count, len(active))):
            r = active.pop(0)
            if r.todo:
                r.step()
                active.append(r)
            else:
                complete(r)

    def begin(c, x, y):
        for kind in range(3):
            to = UNIT * c + 768 * kind
            gw[to : to + 768] = x[:, 128 * kind : 128 * kind + 128].astype(BF)
        for t in range(6):
            to = UNIT * c + 2304 + 128 * t
            gw[to : to + 128] = y[:, 128 * t : 128 * t + 128].astype(BF)
        reduces[c].step()
        active.append(reduces[c])

    g0 = nm
    scr = (ka, va, vat, kt, qa, dk, dv, s_ref, p_ref)
    scr_b = (ka_b, va_b, vat_b, kt_b, qa_b, dk_b, dv_b, s_ref, p_ref)
    sub = iota((R, 128), 0)
    lane = iota((R, 128), 1)
    bias0 = jnp.where(place(sub) < limit, 0.0, NEG)

    def level0(pair, between):
        c = slice(128 * pair, 128 * pair + 128)
        attend_pair(q0t.at[c], do0.at[c], k0[:, c], v0[:, c], bias0, limit, 0, R, o0.at[c], dq0.at[c], scr, between)
        at = 384 * pair
        g0[:, at : at + 128] = flip(dq0[c])
        g0[:, at + 128 : at + 256] = join(dk, 1.0 / LOG2E).astype(BF)
        g0[:, at + 256 : at + 384] = join(dv, 1.0).astype(BF)
        begin(UNITS[0][pair], nn(nmt[...], g0[:, at : at + 384]), nn(o0[c], gp[...]))

    def level2():
        for copy in got_x:
            copy.wait_recv()
        bias = jnp.where(R * (sub >> 6) + 16 * (sub & 63) + mz < kept[0], 0.0, NEG)
        kv = kv2[...].reshape(R, 128).astype(F32)
        prepare_keys(0, 0, 1, kv, kv, bias, ka_b, va_b, vat_b)
        kt_b[...] = jnp.transpose(kv).astype(BF)
        qdt = flip(qd2[...].reshape(256, 128))
        prepare_queries(0, 0, qdt, qa_b)
        col = iota((1, FEW), 1)
        ok = R * (4 * mx + (col >> 6)) + 16 * (col & 63) + mz < kept[0]
        head = Attend(0, 0, 1, False, qa_b[0, :, :FEW], ok, qdt[64:], scr_b)
        attend_one(head)
        o, dq = head.results()
        zb2[:, 1] = flip(jnp.concatenate([o, dq], 0)).reshape(4, 64, 128)
        xb2[...] = jnp.where(lane < 64, dk_b[0] * (1.0 / LOG2E), dv_b[0]).astype(BF).reshape(16, 64, 128)
        got_x[:] = [
            push(xb2.at[pl.ds(4 * (mx ^ k), 4)], xr2.at[k - 1], send2.at[9 + k], recv2.at[9 + k], (0, 4 * k)) for k in (1, 2, 3)
        ]

    got_z = []

    def level2_back():
        for copy in got_x:
            copy.wait_recv()
        total = xb2[plane].astype(F32)
        for k in range(3):
            total += xr2[k].astype(F32)
        zb2[:, 0] = total.astype(BF)
        zr2[mz] = zb2[mz]
        for k in (1, 2, 3):
            got_z.append(push(zb2.at[mz ^ k], zr2.at[mz], send2.at[12 + k], recv2.at[12 + k], (0, k)))

    outs2 = []

    def level2_grads():
        for copy in got_z:
            copy.wait_recv()
        for half in range(2):
            o, dq = blocks_of(zr2[half, 1], zr2[half + 2, 1])
            outs2.append(o.astype(BF))
            gk, gv = blocks_of(zr2[half, 0], zr2[half + 2, 0])
            for kind, x in enumerate((dq, gk, gv)):
                g2[half, :, 128 * kind : 128 * kind + 128] = x.astype(BF)
            begin(UNITS[2][half], nn(nmt[:, fews[half]], g2[half]), nn(jnp.transpose(o).astype(BF), gp[fews[half]]))

    got_back1 = []

    def level1(half):
        rows = halves[half]
        at = place((sub & 511) + 512 * half)
        bias = jnp.where(at < jnp.where(sub < 512, limit, far_limit), 0.0, NEG)
        got1[half].wait_recv()
        k = jnp.concatenate([kv1[half, 0], far1[half, 0]], 0)
        v = jnp.concatenate([kv1[half, 1], far1[half, 1]], 0)
        attend_pair(q1t.at[half], do1.at[half], k, v, bias, limit, 512 * half, 512, o1.at[half], dq1.at[half], scr_b)
        gk = join(dk_b, 1.0 / LOG2E)
        gv = join(dv_b, 1.0)
        near[half, 0] = gk[:512]
        near[half, 1] = gv[:512]
        back[half, 0] = gk[512:].astype(BF)
        back[half, 1] = gv[512:].astype(BF)
        if half == 1:
            level2_back()
        got_back1.append(push(back.at[half], back_r.at[half], send1.at[2 + half], recv1.at[2 + half], (0, 1)))

    def level1_grads(half):
        got_back1[half].wait_recv()
        g1[halves[half], :128] = flip(dq1[half])
        for kind in range(2):
            total = near[half, kind] + back_r[half, kind].astype(F32)
            g1[halves[half], 128 + 128 * kind : 256 + 128 * kind] = total.astype(BF)
        begin(UNITS[1][half], nn(nmt[:, halves[half]], g1[halves[half]]), nn(o1[half], gp[halves[half]]))

    def middle():
        level2_keys()
        level1(0)
        level2()
        level1(1)

    def gap():
        tick(4)
        level1_grads(1)

    level0(0, [(1, middle), (1, None)])
    level2_grads()
    level1_grads(0)
    level0(1, [(1, gap), (1, lambda: tick(5))])
    dk[0, :D] = jnp.zeros((D, 128), F32)

    for half in range(2):
        rows = halves[half]
        at = 768 + 384 * half
        u_ref[...] = nt(g0[rows], wp[:, :768])
        u_ref[...] += nt(g1[rows], wp[:, at : at + 384])
        u_ref[:128] += nt(g2[half], wp[:, 768 + at : 1152 + at])
        tick(2)
        for t in range(4):
            here = slice(512 * half + 128 * t, 512 * half + 128 * t + 128)
            x = xp[here].astype(F32)
            u = u_ref[128 * t : 128 * t + 128] * gain
            cent = x - jnp.mean(x, -1, keepdims=True)
            inv = lax.rsqrt(jnp.mean(cent * cent, -1, keepdims=True) + 1e-05)
            xhat = cent * inv
            mean = jnp.mean(u, -1, keepdims=True)
            dotted = jnp.mean(u * xhat, -1, keepdims=True)
            grad_out[here] = (gp[here].astype(F32) + inv * (u - mean - xhat * dotted)).astype(BF)
        tick(2)
        u_ref[...] = nn(flip(o0[:, rows]), wo[:256]) + nn(flip(o1[half]), wo[256 + 128 * half : 384 + 128 * half])
        u_ref[:128] += nn(outs2[half], wo[512 + 128 * half : 640 + 128 * half])
        tokens[rows] = (xp[rows].astype(F32) + u_ref[...]).astype(BF)
        tick(2)
    store(tokens, layer_hbm)
    store(grad_out, gt_hbm)
    while active:
        tick(1)
    g_gain[...] = (jnp.sum(jnp.transpose(dk[0, :D]), 0, keepdims=True) / gain).reshape(D)
    for copy in sent:
        copy.wait_send()
    for copy in stores:
        copy.wait()


def deliver(
    layer_in, tokens_in, gw_in, gain_in, layer_out, tokens_out, qkv_out, proj_out, gain_out,
    src, gw, dst, qkv, proj, load_sem, store_sem,
):
    loads = [pltpu.make_async_copy(x, src.at[i], load_sem.at[i]) for i, x in enumerate((layer_in, tokens_in))]
    for level in range(3):
        rows = pl.ds(UNIT * UNITS[level][0], 2 * UNIT)
        loads.append(pltpu.make_async_copy(gw_in.at[rows], gw.at[rows], load_sem.at[2 + level]))
    for load in loads:
        load.start()
    stores = []

    def store(x, y):
        stores.append(pltpu.make_async_copy(x, y, store_sem.at[len(stores)]))
        stores[-1].start()

    order = row_order_back()
    for i, out in enumerate((layer_out, tokens_out)):
        loads[i].wait()
        for t in range(4):
            x = jnp.concatenate([src[i, 64 * j + 16 * t : 64 * j + 16 * t + 16] for j in range(16)], 0)
            dst[i, 256 * t : 256 * t + 256] = nn(order, x).astype(BF)
        store(dst.at[i], out)
    heads = head_order()
    for level in range(3):
        loads[2 + level].wait()
        for kind in range(3):
            ats = [UNIT * unit + 768 * kind for unit in UNITS[level]]
            x = jnp.concatenate([gw[at : at + 768] for at in ats], 1)
            x = x.astype(F32) if level == 0 else nn(x, heads)
            c = slice(D * kind + 256 * level, D * kind + 256 * level + 256)
            qkv[:, c] = x
            store(qkv.at[:, c], qkv_out.at[:, c])
        for t in range(6):
            for i, block in enumerate((0, 1, 2, 3) if level == 0 else HEAD_BLOCKS):
                at = UNIT * UNITS[level][i // 2] + 2304 + 128 * t + 64 * (i % 2)
                to = 256 * level + 64 * block
                proj[to : to + 64, 128 * t : 128 * t + 128] = gw[at : at + 64].astype(F32)
        rows = pl.ds(256 * level, 256)
        store(proj.at[rows], proj_out.at[rows])
    gain_out[...] = gain_in[...]
    for copy in stores:
        copy.wait()


def shape(*dims, dtype=BF):
    return jax.ShapeDtypeStruct(dims, dtype)


V = pl.BlockSpec(memory_space=pltpu.VMEM)
S = pl.BlockSpec(memory_space=pltpu.SMEM)
A = pl.BlockSpec(memory_space=pl.ANY)


def vmem(*dims, dtype=BF):
    return pltpu.VMEM(dims, dtype)


def shards(tokens, kept, gain, w, w_out, grad_out):
    dma = pltpu.SemaphoreType.DMA
    layer_p, tokens_p, gw, g_gain = pl.pallas_call(
        layer_kernel,
        out_shape=[shape(R, D), shape(R, D), shape(GRADS, 128), shape(D, dtype=F32)],
        in_specs=[S, V] + [A] * 4,
        out_specs=[A] * 3 + [V],
        scratch_shapes=[
            vmem(R, D), vmem(R, D), vmem(6, D, 256), vmem(R, D), vmem(R, D), vmem(R, D), vmem(D, R),
            vmem(D, 3 * D), vmem(D, D),
            vmem(256, R), vmem(R, 256), vmem(R, 256), vmem(256, R),
            vmem(2, 128, 512), vmem(2, 2, 512, 128), vmem(2, 2, 512, 128), vmem(2, 128, 512),
            vmem(4, 2, 64, 128), vmem(16, 64, 128), vmem(4, 64, 128),
            vmem(256, R), vmem(2, 128, 512), vmem(256, R), vmem(2, 128, 512),
            vmem(R, 384), vmem(2, 128, 384),
            vmem(2, 2, 512, 128, dtype=F32), vmem(2, 2, 512, 128), vmem(2, 2, 512, 128),
            vmem(16, 64, 128), vmem(3, 4, 64, 128), vmem(4, 2, 64, 128), vmem(4, 2, 64, 128),
            vmem(2, R, 128), vmem(2, R, 128), vmem(2, 128, R), vmem(128, R), vmem(2, 128, R),
            vmem(2, R, 128, dtype=F32), vmem(2, R, 128, dtype=F32),
            vmem(2, R, 128), vmem(2, R, 128), vmem(2, 128, R), vmem(128, R), vmem(2, 128, 512),
            vmem(2, R, 128, dtype=F32), vmem(2, R, 128, dtype=F32),
            vmem(2, R, BLK, dtype=F32), vmem(2, R, BLK),
            vmem(GRADS, 128), vmem(GRADS, 128), vmem(GRADS // 2, 128),
            vmem(GRADS * 3 // 8 + 1152, 128), vmem(GRADS // 8 + 384, 128), vmem(GRADS * 3 // 32 + 288, 128),
            vmem(GRADS // 8 + 1152, 128),
            vmem(512, D, dtype=F32),
            dma((25,)), dma((8,)), dma((4,)), dma((4,)), dma((16,)), dma((16,)),
            dma((6, REDUCE_SEMS)), dma((6, REDUCE_SEMS)),
        ],
        compiler_params=pltpu.CompilerParams(vmem_limit_bytes=VMEM, collective_id=0, has_side_effects=True),
        name="layer",
    )(kept, gain, tokens[0], grad_out[0], w, w_out)
    layer, grad_tokens, g_qkv, g_proj, g_gain = pl.pallas_call(
        deliver,
        out_shape=[shape(R, D), shape(R, D), shape(D, 3 * D, dtype=F32), shape(D, D, dtype=F32), shape(D, dtype=F32)],
        in_specs=[A, A, A, V],
        out_specs=[A, A, A, A, V],
        scratch_shapes=[
            vmem(2, R, D), vmem(GRADS, 128), vmem(2, R, D), vmem(D, 3 * D, dtype=F32), vmem(D, D, dtype=F32),
            dma((5,)), dma((14,)),
        ],
        compiler_params=pltpu.CompilerParams(vmem_limit_bytes=VMEM),
        name="deliver",
    )(layer_p, tokens_p, gw, g_gain)
    return layer[None], grad_tokens[None], g_qkv, g_proj, g_gain


def solution(mesh):
    in_specs = (P("dp", "ctx", None), P("dp"), P(), P(), P(), P("dp", "ctx", None))
    out_specs = (P("dp", "ctx", None), P("dp", "ctx", None), P(), P(), P())
    return jax.shard_map(shards, mesh=mesh, in_specs=in_specs, out_specs=out_specs, check_vma=False)
```
